256 devices in a mesh: group: 32 (over x, y, core), dev: 8 (over z).
Axes of the slice: x: 4, y: 4, z: 8, core: 2. Of those that a mesh axis runs over, the one named last changes fastest.
Arguments:
- embeddings: bfloat16 [524288, 1024], P(('group', 'dev')), may hold values from -0.28125 to 0.28125
- nearest: float32 [524288], P(('group', 'dev')), may hold values from 0.5 to 32
- chosen: int32 [2, 512], replicated, may hold values from 0 to 524287, as said below
Outputs:
- nearest_after: float32 [524288], P(('group', 'dev'))
- round_costs: float32 [2], replicated
The draws below stay inside these ranges and needn't reach their ends.
Inputs may be any that keep to these rules, and one draw needn't show every extreme that they name: `chosen`: in each round every device's rows (an aligned block of 2048 rows) hold at most 6 of the picks, and some device holds exactly 6; a row may be picked twice.
All inputs are finite; a program needn't handle non-finite values.
Results may differ from the reference program's by a relative error of at most 0.0003.
Values may be sent and summed in bfloat16 or wider, within the bound.
A program may use at most 64 MiB of HBM per device.

```python
import jax
import jax.numpy as jnp
from jax import lax

D = 1024
ROWS_DEV = 2048
CANDS = 512
ROUNDS = 2
MOST = 6
ROWS = 524288
N_GROUP = 32
N_DEV = 8


def draw_embeddings(key, part):
    key = jax.random.fold_in(key, 5)
    clusters = 2 * CANDS
    key_member = jax.random.fold_in(key, 1)
    key_centre = jax.random.fold_in(key, 2)
    key_noise = jax.random.fold_in(key, 3)
    key_scale = jax.random.fold_in(key, 4)
    member = jax.random.randint(key_member, (ROWS,), 0, clusters)
    position = jnp.arange(ROWS).astype(jnp.float32)
    widen = 0.2 * (1.0 + 3.0 * position / ROWS)
    scales = jax.random.uniform(key_scale, (clusters, 1), jnp.float32, 0.75, 1.25)
    centres = jnp.clip(jax.random.normal(key_centre, (clusters, D), jnp.float32), -4.0, 4.0)
    noise = jnp.clip(jax.random.normal(key_noise, (ROWS, D), jnp.float32), -4.0, 4.0)
    rows = (centres * scales)[member] + widen[:, None] * noise
    return (rows * D ** (-0.5)).astype(jnp.bfloat16)


def draw_nearest(key, part):
    key = jax.random.fold_in(key, 11)
    position = jnp.arange(ROWS).astype(jnp.float32)
    rising = 1.0 + 2.0 * position / ROWS
    spread = jax.random.uniform(key, (ROWS,), jnp.float32, 0.5, 3.5)
    return spread * rising


def draw_chosen(key, part):
    key = jax.random.fold_in(key, 7)
    devices = N_GROUP * N_DEV
    rounds_out = []
    for step in range(ROUNDS):
        round_key = jax.random.fold_in(key, step)
        key_first = jax.random.fold_in(round_key, 1)
        key_slots = jax.random.fold_in(round_key, 2)
        key_within = jax.random.fold_in(round_key, 3)
        key_order = jax.random.fold_in(round_key, 4)
        fullest = jax.random.randint(key_first, (), 0, devices)
        slots = jax.random.permutation(key_slots, (devices - 1) * MOST)[:CANDS - MOST]
        others = slots // MOST
        others = others + (others >= fullest).astype(jnp.int32)
        owning = jnp.concatenate([jnp.full((MOST,), fullest, jnp.int32), others.astype(jnp.int32)])
        within = jax.random.randint(key_within, (CANDS,), 0, ROWS_DEV)
        picked = owning * ROWS_DEV + within
        order = jax.random.permutation(key_order, CANDS)
        rounds_out.append(picked[order])
    return jnp.stack(rounds_out).astype(jnp.int32)


def setup_inputs(seed: int = 0) -> dict:
    arg_keys = jax.random.split(jax.random.key(seed), 4)
    return {
        "embeddings": draw_embeddings(jax.random.fold_in(arg_keys[3], 71), 0),
        "nearest": draw_nearest(jax.random.fold_in(arg_keys[3], 71), 0),
        "chosen": draw_chosen(jax.random.fold_in(arg_keys[3], 71), 0),
    }


def reference(embeddings, nearest, chosen):
    row_norms = jnp.sum(jnp.square(embeddings.astype(jnp.float32)), axis=1)
    blocks_x = embeddings.reshape(-1, ROWS_DEV, D)
    blocks_n = row_norms.reshape(-1, ROWS_DEV)
    costs = []
    for step in range(ROUNDS):
        candidates = embeddings[chosen[step]]
        cand_norm = jnp.sum(jnp.square(candidates.astype(jnp.float32)), axis=1)

        def update(items):
            block_x, block_n, block_d = items
            products = jnp.dot(block_x, candidates.T, preferred_element_type=jnp.float32)
            distance = jnp.maximum((block_n[:, None] + cand_norm[None, :]) - 2.0 * products, 0.0)
            return jnp.minimum(block_d, jnp.min(distance, axis=1))

        nearest = lax.map(update, (blocks_x, blocks_n, nearest.reshape(-1, ROWS_DEV))).reshape(-1)
        costs.append(jnp.sum(nearest) / ROWS)
    return nearest, jnp.stack(costs)
```

```python
import functools

import jax
import jax.numpy as jnp
from jax import lax
from jax.experimental import pallas as pl
from jax.experimental.pallas import tpu as pltpu
from jax.sharding import PartitionSpec as P

MESH = pl.DeviceIdType.MESH
NT = (((1,), (1,)), ((), ()))
NX, NY = 4, 4
MOST = 6
FAR = 2.0**50
NONE = 2**30
TILE = 256


def place():
    group = lax.axis_index("group")
    return group // (2 * NY), (group // 2) % NY, group % 2, lax.axis_index("dev")


def device(x, y, c, z):
    return ((x * NY + y) * 2 + c, z)


def picked_rows(chosen_ref, emb_ref, position):
    rows = emb_ref.shape[0] * 16
    cands = chosen_ref.shape[1]
    chosen = chosen_ref[...]
    order = lax.broadcasted_iota(jnp.int32, chosen.shape, 1)
    within = chosen - position * rows
    owned = (within >= 0) & (within < rows)
    key = jnp.where(owned, within * cands + order, NONE)
    found = [[], []]
    line = lax.broadcasted_iota(jnp.int32, (16, emb_ref.shape[2]), 0)
    for _ in range(MOST):
        least = jnp.min(key, axis=1, keepdims=True)
        key = jnp.where(key == least, NONE, key)
        tile = jnp.minimum(least, rows * cands - 1) // (16 * cands)
        inside = least // cands - tile * 16
        for turn in range(2):
            block = emb_ref[tile[turn, 0]].astype(jnp.float32)
            chosen_line = line == inside[turn : turn + 1, :]
            row = jnp.sum(jnp.where(chosen_line, block, 0.0), axis=0, keepdims=True)
            found[turn].append(jnp.where(least[turn : turn + 1, :] < NONE, row * -2.0, FAR))
    return found


def kernel(
    chosen_ref, near_ref, emb_hbm, out_ref, cost_ref,
    emb, col, cand, least, sum_z, sum_xy,
    emb_sem, zs, zr, bs, cs, ks, slab_r, sib_r, azs, azr, axs, axr, total_rows,
):
    x, y, c, z = place()
    nz = lax.axis_size("dev")
    position = lax.axis_index("group") * nz + z
    rows = emb.shape[0] * 16
    slab = nz * MOST
    major, minor = (y, x), (x, y)

    load = pltpu.make_async_copy(emb_hbm, emb, emb_sem)
    load.start()

    column = [((z + dz) % nz, (c + dc) % 2) for dz in range(nz) for dc in range(2) if dz or dc]
    plane = [((x + dx) % NX, (y + dy) % NY) for dx in range(NX) for dy in range(NY) if dx or dy]
    barrier = pltpu.get_barrier_semaphore()
    for tz, tc in column:
        pl.semaphore_signal(barrier, inc=1, device_id=device(x, y, tc, tz), device_id_type=MESH)
    for tx, ty in plane:
        pl.semaphore_signal(barrier, inc=1, device_id=device(tx, ty, c, z), device_id_type=MESH)

    least[...] = jnp.full(least.shape, jnp.inf, jnp.float32)
    load.wait()
    found = picked_rows(chosen_ref, emb, position)
    pad = jnp.zeros((4, emb.shape[2]), jnp.float32)
    col[z] = jnp.concatenate(found[0] + found[1] + [pad], axis=0).astype(jnp.bfloat16)
    pl.semaphore_wait(barrier, len(column) + len(plane))

    def z_copy(k):
        return pltpu.make_async_remote_copy(
            src_ref=col.at[z], dst_ref=col.at[z], send_sem=zs.at[k - 1], recv_sem=zr.at[z],
            device_id=device(x, y, c, (z + k) % nz), device_id_type=MESH)

    def z_arrival(k):
        t = (z + k) % nz
        return pltpu.make_async_remote_copy(
            src_ref=col.at[t], dst_ref=col.at[t], send_sem=zs.at[k - 1], recv_sem=zr.at[t],
            device_id=device(x, y, c, t), device_id_type=MESH)

    for k in (4, 3, 5, 2, 6, 1, 7):
        z_copy(k).start()

    for j in range(rows // 128):
        part = emb[8 * j : 8 * (j + 1)].reshape(128, -1).astype(jnp.float32)
        part = part * part
        part = sum(part[:, 128 * i : 128 * (i + 1)] for i in range(part.shape[1] // 128))
        out_ref[:, 128 * j : 128 * (j + 1)] = jnp.sum(part.T, axis=0, keepdims=True)

    for k in range(1, nz):
        z_arrival(k).wait_recv()

    whole = [col[t].astype(jnp.float32) for t in range(nz)]
    for p in range(2):
        packed = jnp.concatenate([w[MOST * p : MOST * (p + 1), :] for w in whole], axis=0)
        start = pl.multiple_of((minor[p] * 2 + c) * slab, 16)
        cand[p, major[p], pl.ds(start, slab), :] = packed.astype(jnp.bfloat16)

    def slab_at(p, a, b, core):
        start = pl.multiple_of((b * 2 + core) * slab, 16)
        return cand.at[p, a, pl.ds(start, slab), :]

    def spot(p, a, b):
        return (b, a) if p == 0 else (a, b)

    def copy(p, a, b, core, ssem, rsem, target):
        ref = slab_at(p, a, b, core)
        return pltpu.make_async_remote_copy(
            src_ref=ref, dst_ref=ref, send_sem=ssem, recv_sem=rsem,
            device_id=target, device_id_type=MESH)

    def major_copy(p, k):
        a, b = major[p], minor[p]
        tx, ty = spot(p, (a + k) % 4, b)
        return copy(p, a, b, c, bs.at[p, k - 1], slab_r.at[p, a, b], device(tx, ty, c, z))

    def minor_copy(p, a, k):
        b = minor[p]
        tx, ty = spot(p, major[p], (b + k) % 4)
        return copy(p, a, b, c, cs.at[p, a, k - 1], slab_r.at[p, a, b], device(tx, ty, c, z))

    def core_copy(p, a, b):
        return copy(p, a, b, c, ks.at[p, a, b], sib_r.at[p, a, b], device(x, y, 1 - c, z))

    def slab_arrival(p, a, b):
        return copy(p, a, b, c, ks.at[p, a, b], slab_r.at[p, a, b], device(x, y, 1 - c, z))

    def core_arrival(p, a, b):
        return copy(p, a, b, 1 - c, ks.at[p, a, b], sib_r.at[p, a, b], device(x, y, 1 - c, z))

    for k in (2, 1, 3):
        for p in range(2):
            major_copy(p, k).start()
    for p in range(2):
        for k in (2, 1, 3):
            minor_copy(p, major[p], k).start()
        core_copy(p, major[p], minor[p]).start()
    for k in (1, 3, 2):
        for p in range(2):
            a = (major[p] + k) % 4
            slab_arrival(p, a, minor[p]).wait_recv()
            for j in (2, 1, 3):
                minor_copy(p, a, j).start()
            core_copy(p, a, minor[p]).start()

    def turn_at(p, k):
        return (major[p] + k + (k // 2) * (1 - 2 * (k % 2))) % 4

    def pass_on(p, k):
        a = turn_at(p, k)
        for j in (1, 3, 2):
            b = (minor[p] + j) % 4
            slab_arrival(p, a, b).wait_recv()
            core_copy(p, a, b).start()

    def absorb(p, k):
        a = turn_at(p, k)
        for b in range(4):
            core_arrival(p, a, b).wait_recv()
        block = cand[p, a]
        wide = block.astype(jnp.float32)
        norm = jnp.sum(wide * wide, axis=1, keepdims=True) * 0.25
        for j in range(rows // TILE):
            lanes = slice(TILE * j, TILE * (j + 1))
            mine = emb[TILE // 16 * j : TILE // 16 * (j + 1)].reshape(TILE, -1)
            product = lax.dot_general(block, mine, NT, preferred_element_type=jnp.float32)
            reach = (product + norm).reshape(-1, 8, TILE)
            least[p, :, lanes] = jnp.minimum(least[p, :, lanes], jnp.min(reach, axis=0))

    for p in range(2):
        pass_on(p, 0)

    def step(k, _):
        for p in range(2):
            absorb(p, k)

            @pl.when(k < 3)
            def _():
                pass_on(p, k + 1)

        return 0

    lax.fori_loop(0, 4, step, 0)

    norms = out_ref[...]
    near = near_ref[...]
    sums = []
    for p in range(2):
        reach = jnp.min(least[p], axis=0, keepdims=True)
        near = jnp.minimum(near, jnp.maximum(norms + reach, 0.0))
        sums.append(jnp.sum(near, axis=1, keepdims=True))
    lane = lax.broadcasted_iota(jnp.int32, (1, 128), 1)
    share = jnp.where(lane == 0, sums[0], jnp.where(lane == 1, sums[1], 0.0))

    at_z = z * 2 + c
    sum_z[at_z] = share
    for i, (tz, tc) in enumerate(column):
        pltpu.make_async_remote_copy(
            src_ref=sum_z.at[at_z], dst_ref=sum_z.at[at_z], send_sem=azs.at[i],
            recv_sem=azr.at[at_z], device_id=device(x, y, tc, tz), device_id_type=MESH).start()
    out_ref[...] = near
    for i, (tz, tc) in enumerate(column):
        t = tz * 2 + tc
        pltpu.make_async_remote_copy(
            src_ref=sum_z.at[t], dst_ref=sum_z.at[t], send_sem=azs.at[i],
            recv_sem=azr.at[t], device_id=device(x, y, tc, tz), device_id_type=MESH).wait_recv()
    at_xy = x * NY + y
    sum_xy[at_xy] = jnp.sum(sum_z[...], axis=0)
    for i, (tx, ty) in enumerate(plane):
        pltpu.make_async_remote_copy(
            src_ref=sum_xy.at[at_xy], dst_ref=sum_xy.at[at_xy], send_sem=axs.at[i],
            recv_sem=axr.at[at_xy], device_id=device(tx, ty, c, z), device_id_type=MESH).start()

    for k in range(1, nz):
        z_copy(k).wait_send()
    for p in range(2):
        for k in (1, 2, 3):
            major_copy(p, k).wait_send()
        for a in range(4):
            for k in (1, 2, 3):
                minor_copy(p, a, k).wait_send()
            for b in range(4):
                core_copy(p, a, b).wait_send()
    for i, (tz, tc) in enumerate(column):
        pltpu.make_async_remote_copy(
            src_ref=sum_z.at[at_z], dst_ref=sum_z.at[at_z], send_sem=azs.at[i],
            recv_sem=azr.at[at_z], device_id=device(x, y, tc, tz), device_id_type=MESH).wait_send()

    for i, (tx, ty) in enumerate(plane):
        t = tx * NY + ty
        both = pltpu.make_async_remote_copy(
            src_ref=sum_xy.at[t], dst_ref=sum_xy.at[t], send_sem=axs.at[i],
            recv_sem=axr.at[t], device_id=device(tx, ty, c, z), device_id_type=MESH)
        both.wait_recv()
        both.wait_send()
    final = jnp.sum(sum_xy[...], axis=0) / total_rows
    cost_ref[0] = final[0, 0]
    cost_ref[1] = final[0, 1]


def local(embeddings, nearest, chosen):
    rows, width = embeddings.shape
    nz = lax.axis_size("dev")
    total_rows = rows * nz * lax.axis_size("group")
    dma = pltpu.SemaphoreType.DMA

    near, cost = pl.pallas_call(
        functools.partial(kernel, total_rows=total_rows),
        out_shape=(
            jax.ShapeDtypeStruct((1, rows), jnp.float32),
            jax.ShapeDtypeStruct((2,), jnp.float32),
        ),
        in_specs=[
            pl.BlockSpec(memory_space=pltpu.VMEM),
            pl.BlockSpec(memory_space=pltpu.VMEM),
            pl.BlockSpec(memory_space=pl.ANY),
        ],
        out_specs=(
            pl.BlockSpec(memory_space=pltpu.VMEM),
            pl.BlockSpec(memory_space=pltpu.SMEM),
        ),
        scratch_shapes=[
            pltpu.VMEM((rows // 16, 16, width), jnp.bfloat16),
            pltpu.VMEM((nz, 16, width), jnp.bfloat16),
            pltpu.VMEM((2, 4, 8 * nz * MOST, width), jnp.bfloat16),
            pltpu.VMEM((2, 8, rows), jnp.float32),
            pltpu.VMEM((2 * nz, 1, 128), jnp.float32),
            pltpu.VMEM((NX * NY, 1, 128), jnp.float32),
            dma,
            dma((nz - 1,)),
            dma((nz,)),
            dma((2, 3)),
            dma((2, 4, 3)),
            dma((2, 4, 4)),
            dma((2, 4, 4)),
            dma((2, 4, 4)),
            dma((2 * nz - 1,)),
            dma((2 * nz,)),
            dma((NX * NY - 1,)),
            dma((NX * NY,)),
        ],
        compiler_params=pltpu.CompilerParams(
            collective_id=0, has_side_effects=True, vmem_limit_bytes=40 * 2**20
        ),
        cost_estimate=pl.CostEstimate(
            flops=2 * rows * width * 3072, bytes_accessed=rows * width * 2, transcendentals=0
        ),
    )(chosen, nearest.reshape(1, rows), embeddings.reshape(rows // 16, 16, width))
    return near.reshape(rows), cost


def solution(mesh):
    return jax.shard_map(
        local,
        mesh=mesh,
        in_specs=(P(("group", "dev"), None), P(("group", "dev")), P()),
        out_specs=(P(("group", "dev")), P()),
        check_vma=False,
    )
```

```python
import functools

import jax
import jax.numpy as jnp
from jax import lax
from jax.experimental import pallas as pl
from jax.experimental.pallas import tpu as pltpu
from jax.sharding import PartitionSpec as P

MESH = pl.DeviceIdType.MESH
NT = (((1,), (1,)), ((), ()))
NX, NY = 4, 4
MOST = 6
NONE = 2**30
TILE = 256


def place():
    group = lax.axis_index("group")
    return group // (2 * NY), (group // 2) % NY, group % 2, lax.axis_index("dev")


def device(x, y, c, z):
    return ((x * NY + y) * 2 + c, z)


def find_picks(chosen, position, rows):
    cands = chosen.shape[1]
    order = lax.broadcasted_iota(jnp.int32, chosen.shape, 1)
    within = chosen - position * rows
    owned = (within >= 0) & (within < rows)
    key = jnp.where(owned, within * cands + order, NONE)
    found = []
    for _ in range(MOST):
        least = jnp.min(key, axis=1, keepdims=True)
        key = jnp.where(key == least, NONE, key)
        index = jnp.minimum(least, rows * cands - 1) // cands
        tile = index // 16
        found.append((tile, index - tile * 16))
    return found


def picked_rows(found, emb_ref):
    line = lax.broadcasted_iota(jnp.int32, (16, emb_ref.shape[2]), 0)
    picked = []
    for turn in range(2):
        for tile, inside in found:
            block = emb_ref[tile[turn, 0]].astype(jnp.float32)
            here = line == inside[turn : turn + 1, :]
            picked.append(jnp.sum(jnp.where(here, block, 0.0), axis=0, keepdims=True) * -2.0)
    return jnp.concatenate(picked, axis=0)


def slot_sources(chosen_ref, x, y, z, rows, nz):
    cands = chosen_ref.shape[1]
    per = 2 * cands // nz
    turn = z // (nz // 2)
    start = (z % (nz // 2)) * per
    every = chosen_ref[0:1, :] * (1 - turn) + chosen_ref[1:2, :] * turn
    order = lax.broadcasted_iota(jnp.int32, (per, cands), 1)
    place_in = lax.broadcasted_iota(jnp.int32, (per, cands), 0) + start
    mine = jnp.sum(jnp.where(order == place_in, every, 0), axis=1, keepdims=True)
    owner = mine // rows
    earlier = (every < mine) | ((every == mine) & (order < place_in))
    rank = jnp.sum(jnp.where((every // rows == owner) & earlier, 1, 0), axis=1, keepdims=True)
    slot = turn * MOST + rank
    group = owner // nz
    source = ((owner - group * nz) * 2 + group % 2) * 16
    here = group // 2 == x * NY + y
    lane = lax.broadcasted_iota(jnp.int32, (per, 32 * nz), 1)
    main = (here & (lane == source + slot)).astype(jnp.bfloat16)
    low = here & (lane == source + 12 + slot % 4)
    tails = [(low & (slot // 4 == i)).astype(jnp.bfloat16) for i in range(3)]
    return main, tails


def kernel(
    chosen_hbm, near_hbm, emb_hbm, out_ref, cost_ref,
    chosen_ref, near_ref, emb, sent, col, parts, shares, ours, cand, least, sum_z, sum_xy,
    in_sem, zs, zr, ps, pr, os, orr, bs, cs, ks, slab_r, sib_r, azs, azr, axs, axr, total_rows,
):
    x, y, c, z = place()
    nz = lax.axis_size("dev")
    position = lax.axis_index("group") * nz + z
    rows = emb.shape[0] * 16
    slab = 4 * nz
    half = emb.shape[2] // 2
    cut = 3 * half // 4
    at_z, at_xy = z * 2 + c, x * NY + y
    major, minor = (y, x), (x, y)

    load = pltpu.make_async_copy(emb_hbm, emb, in_sem.at[0])
    load_chosen = pltpu.make_async_copy(chosen_hbm, chosen_ref, in_sem.at[1])
    load_near = pltpu.make_async_copy(near_hbm, near_ref, in_sem.at[2])
    load_chosen.start()
    load.start()
    load_near.start()

    column = [((z + dz) % nz, (c + dc) % 2) for dz in range(nz) for dc in range(2) if dz or dc]
    plane = [((x + dx) % NX, (y + dy) % NY) for dx in range(NX) for dy in range(NY) if dx or dy]
    barrier = pltpu.get_barrier_semaphore()
    for tz, tc in column:
        pl.semaphore_signal(barrier, inc=1, device_id=device(x, y, tc, tz), device_id_type=MESH)
    for tx, ty in plane:
        pl.semaphore_signal(barrier, inc=1, device_id=device(tx, ty, c, z), device_id_type=MESH)

    least[...] = jnp.full(least.shape, jnp.inf, jnp.float32)
    load_chosen.wait()
    picks = find_picks(chosen_ref[...], position, rows)
    load.wait()
    found = picked_rows(picks, emb)
    for h in range(2):
        wide = found[:, half * h : half * (h + 1)]
        tail = jnp.concatenate([wide[4 * i : 4 * i + 4, cut:] for i in range(3)], axis=1)
        sent[h] = jnp.concatenate([wide[:, :cut], tail], axis=0).astype(jnp.bfloat16)
    col[at_z] = sent[c]
    pl.semaphore_wait(barrier, len(column) + len(plane))

    def remote(src, dst, ssem, rsem, target):
        return pltpu.make_async_remote_copy(
            src_ref=src, dst_ref=dst, send_sem=ssem, recv_sem=rsem,
            device_id=target, device_id_type=MESH)

    def slots_copy(i):
        tz, tc = column[i]
        return remote(sent.at[tc], col.at[at_z], zs.at[i], zr.at[at_z], device(x, y, tc, tz))

    def slots_arrival(i):
        tz, tc = column[i]
        t = tz * 2 + tc
        return remote(sent.at[tc], col.at[t], zs.at[i], zr.at[t], device(x, y, tc, tz))

    far_first = sorted(range(len(column)), key=lambda i: abs((i + 1) // 2 - nz // 2))
    for i in far_first:
        slots_copy(i).start()

    for j in range(rows // 128):
        part = emb[8 * j : 8 * (j + 1)].reshape(128, -1).astype(jnp.float32)
        part = part * part
        part = sum(part[:, 128 * i : 128 * (i + 1)] for i in range(part.shape[1] // 128))
        out_ref[:, 128 * j : 128 * (j + 1)] = jnp.sum(part.T, axis=0, keepdims=True)

    main, tails = slot_sources(chosen_ref, x, y, z, rows, nz)
    for i in range(len(column)):
        slots_arrival(i).wait_recv()

    gathered = col[...].reshape(-1, cut)
    left = jnp.dot(main, gathered, preferred_element_type=jnp.float32)
    right = sum(
        jnp.dot(tail, gathered[:, 128 * i : 128 * (i + 1)], preferred_element_type=jnp.float32)
        for i, tail in enumerate(tails)
    )
    dense = jnp.concatenate([left, right], axis=1)
    for t in range(NX * NY):
        rows8 = dense[8 * t : 8 * t + 8]
        both = jnp.concatenate([rows8[:, : half // 2], rows8[:, half // 2 :]], axis=0)
        parts[t] = both.astype(jnp.bfloat16)
    shares[at_xy] = parts[at_xy]

    def part_copy(i):
        tx, ty = plane[i]
        t = tx * NY + ty
        return remote(parts.at[t], shares.at[at_xy], ps.at[i], pr.at[at_xy], device(tx, ty, c, z))

    def part_arrival(i):
        tx, ty = plane[i]
        t = tx * NY + ty
        return remote(parts.at[t], shares.at[t], ps.at[i], pr.at[t], device(tx, ty, c, z))

    for i in range(len(plane)):
        part_copy(i).start()
    for i in range(len(plane)):
        part_arrival(i).wait_recv()
    ours[z] = jnp.sum(shares[...].astype(jnp.float32), axis=0).astype(jnp.bfloat16)

    def z_copy(k):
        return remote(ours.at[z], ours.at[z], os.at[k - 1], orr.at[z], device(x, y, c, (z + k) % nz))

    def z_arrival(k):
        t = (z + k) % nz
        return remote(ours.at[t], ours.at[t], os.at[k - 1], orr.at[t], device(x, y, c, t))

    for k in (4, 3, 5, 2, 6, 1, 7):
        z_copy(k).start()
    for k in range(1, nz):
        z_arrival(k).wait_recv()
    for p in range(2):
        rows8 = [ours[p * (nz // 2) + t].astype(jnp.float32) for t in range(nz // 2)]
        packed = [jnp.concatenate([r[:8], r[8:]], axis=1) for r in rows8]
        start = pl.multiple_of(minor[p] * slab, 16)
        cand[p, c, major[p], pl.ds(start, slab), :] = jnp.concatenate(packed, axis=0).astype(
            jnp.bfloat16
        )

    def slab_at(p, a, b, core):
        start = pl.multiple_of(b * slab, 16)
        return cand.at[p, core, a, pl.ds(start, slab), :]

    def spot(p, a, b):
        return (b, a) if p == 0 else (a, b)

    def copy(p, a, b, core, ssem, rsem, target):
        ref = slab_at(p, a, b, core)
        return remote(ref, ref, ssem, rsem, target)

    def major_copy(p, k):
        a, b = major[p], minor[p]
        tx, ty = spot(p, (a + k) % 4, b)
        return copy(p, a, b, c, bs.at[p, k - 1], slab_r.at[p, a, b], device(tx, ty, c, z))

    def minor_copy(p, a, k):
        b = minor[p]
        tx, ty = spot(p, major[p], (b + k) % 4)
        return copy(p, a, b, c, cs.at[p, a, k - 1], slab_r.at[p, a, b], device(tx, ty, c, z))

    def core_copy(p, a, b):
        return copy(p, a, b, c, ks.at[p, a, b], sib_r.at[p, a, b], device(x, y, 1 - c, z))

    def slab_arrival(p, a, b):
        return copy(p, a, b, c, ks.at[p, a, b], slab_r.at[p, a, b], device(x, y, 1 - c, z))

    def core_arrival(p, a, b):
        return copy(p, a, b, 1 - c, ks.at[p, a, b], sib_r.at[p, a, b], device(x, y, 1 - c, z))

    for k in (2, 1, 3):
        for p in range(2):
            major_copy(p, k).start()
    for p in range(2):
        for k in (2, 1, 3):
            minor_copy(p, major[p], k).start()
        core_copy(p, major[p], minor[p]).start()
    for k in (1, 3, 2):
        for p in range(2):
            a = (major[p] + k) % 4
            slab_arrival(p, a, minor[p]).wait_recv()
            for j in (2, 1, 3):
                minor_copy(p, a, j).start()
            core_copy(p, a, minor[p]).start()

    def pass_on(p, k):
        a = (major[p] + k) % 4
        for j in (1, 3, 2):
            b = (minor[p] + j) % 4
            slab_arrival(p, a, b).wait_recv()
            core_copy(p, a, b).start()

    def absorb(p, ks_):
        at = [(major[p] + k) % 4 for k in ks_]
        for a in at:
            for b in range(4):
                core_arrival(p, a, b).wait_recv()
        blocks = [jnp.concatenate([cand[p, h, a] for a in at], axis=0) for h in range(2)]
        wide = [block.astype(jnp.float32) for block in blocks]
        norm = jnp.sum(wide[0] * wide[0] + wide[1] * wide[1], axis=1, keepdims=True) * 0.25
        for j in range(rows // TILE):
            lanes = slice(TILE * j, TILE * (j + 1))
            mine = emb[TILE // 16 * j : TILE // 16 * (j + 1)].reshape(TILE, -1)
            product = sum(
                lax.dot_general(
                    blocks[h], mine[:, half * h : half * (h + 1)], NT,
                    preferred_element_type=jnp.float32)
                for h in range(2)
            )
            reach = (product + norm).reshape(-1, 8, TILE)
            least[p, :, lanes] = jnp.minimum(least[p, :, lanes], jnp.min(reach, axis=0))

    for k in (0, 1):
        for p in range(2):
            pass_on(p, k)
    absorb(0, (0, 1))
    pass_on(0, 3)
    pass_on(1, 3)
    absorb(1, (0, 1))
    pass_on(0, 2)
    pass_on(1, 2)
    absorb(0, (3, 2))
    absorb(1, (3, 2))
    load_near.wait()

    norms = out_ref[...]
    near = near_ref[...]
    sums = []
    for p in range(2):
        reach = jnp.min(least[p], axis=0, keepdims=True)
        near = jnp.minimum(near, jnp.maximum(norms + reach, 0.0))
        sums.append(jnp.sum(near, axis=1, keepdims=True))
    lane = lax.broadcasted_iota(jnp.int32, (1, 128), 1)
    share = jnp.where(lane == 0, sums[0], jnp.where(lane == 1, sums[1], 0.0))

    sum_z[at_z] = share
    for i, (tz, tc) in enumerate(column):
        pltpu.make_async_remote_copy(
            src_ref=sum_z.at[at_z], dst_ref=sum_z.at[at_z], send_sem=azs.at[i],
            recv_sem=azr.at[at_z], device_id=device(x, y, tc, tz), device_id_type=MESH).start()
    out_ref[...] = near
    for i, (tz, tc) in enumerate(column):
        t = tz * 2 + tc
        pltpu.make_async_remote_copy(
            src_ref=sum_z.at[t], dst_ref=sum_z.at[t], send_sem=azs.at[i],
            recv_sem=azr.at[t], device_id=device(x, y, tc, tz), device_id_type=MESH).wait_recv()
    sum_xy[at_xy] = jnp.sum(sum_z[...], axis=0)
    for i, (tx, ty) in enumerate(plane):
        pltpu.make_async_remote_copy(
            src_ref=sum_xy.at[at_xy], dst_ref=sum_xy.at[at_xy], send_sem=axs.at[i],
            recv_sem=axr.at[at_xy], device_id=device(tx, ty, c, z), device_id_type=MESH).start()

    for i in range(len(column)):
        slots_copy(i).wait_send()
    for i in range(len(plane)):
        part_copy(i).wait_send()
    for k in range(1, nz):
        z_copy(k).wait_send()
    for p in range(2):
        for k in (1, 2, 3):
            major_copy(p, k).wait_send()
        for a in range(4):
            for k in (1, 2, 3):
                minor_copy(p, a, k).wait_send()
            for b in range(4):
                core_copy(p, a, b).wait_send()
    for i, (tz, tc) in enumerate(column):
        pltpu.make_async_remote_copy(
            src_ref=sum_z.at[at_z], dst_ref=sum_z.at[at_z], send_sem=azs.at[i],
            recv_sem=azr.at[at_z], device_id=device(x, y, tc, tz), device_id_type=MESH).wait_send()

    for i, (tx, ty) in enumerate(plane):
        t = tx * NY + ty
        both = pltpu.make_async_remote_copy(
            src_ref=sum_xy.at[t], dst_ref=sum_xy.at[t], send_sem=axs.at[i],
            recv_sem=axr.at[t], device_id=device(tx, ty, c, z), device_id_type=MESH)
        both.wait_recv()
        both.wait_send()
    final = jnp.sum(sum_xy[...], axis=0) / total_rows
    cost_ref[0] = final[0, 0]
    cost_ref[1] = final[0, 1]


def local(embeddings, nearest, chosen):
    rows, width = embeddings.shape
    nz = lax.axis_size("dev")
    total_rows = rows * nz * lax.axis_size("group")
    dma = pltpu.SemaphoreType.DMA

    near, cost = pl.pallas_call(
        functools.partial(kernel, total_rows=total_rows),
        out_shape=(
            jax.ShapeDtypeStruct((1, rows), jnp.float32),
            jax.ShapeDtypeStruct((2,), jnp.float32),
        ),
        in_specs=[
            pl.BlockSpec(memory_space=pl.ANY),
            pl.BlockSpec(memory_space=pl.ANY),
            pl.BlockSpec(memory_space=pl.ANY),
        ],
        out_specs=(
            pl.BlockSpec(memory_space=pltpu.VMEM),
            pl.BlockSpec(memory_space=pltpu.SMEM),
        ),
        scratch_shapes=[
            pltpu.VMEM(chosen.shape, jnp.int32),
            pltpu.VMEM((1, rows), jnp.float32),
            pltpu.VMEM((rows // 16, 16, width), jnp.bfloat16),
            pltpu.VMEM((2, 16, 3 * width // 8), jnp.bfloat16),
            pltpu.VMEM((2 * nz, 16, 3 * width // 8), jnp.bfloat16),
            pltpu.VMEM((NX * NY, 16, width // 4), jnp.bfloat16),
            pltpu.VMEM((NX * NY, 16, width // 4), jnp.bfloat16),
            pltpu.VMEM((nz, 16, width // 4), jnp.bfloat16),
            pltpu.VMEM((2, 2, 4, 16 * nz, width // 2), jnp.bfloat16),
            pltpu.VMEM((2, 8, rows), jnp.float32),
            pltpu.VMEM((2 * nz, 1, 128), jnp.float32),
            pltpu.VMEM((NX * NY, 1, 128), jnp.float32),
            dma((3,)),
            dma((2 * nz - 1,)),
            dma((2 * nz,)),
            dma((NX * NY - 1,)),
            dma((NX * NY,)),
            dma((nz - 1,)),
            dma((nz,)),
            dma((2, 3)),
            dma((2, 4, 3)),
            dma((2, 4, 4)),
            dma((2, 4, 4)),
            dma((2, 4, 4)),
            dma((2 * nz - 1,)),
            dma((2 * nz,)),
            dma((NX * NY - 1,)),
            dma((NX * NY,)),
        ],
        compiler_params=pltpu.CompilerParams(
            collective_id=0, has_side_effects=True, vmem_limit_bytes=60 * 2**20
        ),
        cost_estimate=pl.CostEstimate(
            flops=4 * rows * width * chosen.shape[1], bytes_accessed=rows * width * 2, transcendentals=0
        ),
    )(chosen, nearest.reshape(1, rows), embeddings.reshape(rows // 16, 16, width))
    return near.reshape(rows), cost


def solution(mesh):
    return jax.shard_map(
        local,
        mesh=mesh,
        in_specs=(P(("group", "dev"), None), P(("group", "dev")), P()),
        out_specs=(P(("group", "dev")), P()),
        check_vma=False,
    )
```

```python
import functools

import jax
import jax.numpy as jnp
from jax import lax
from jax.experimental import pallas as pl
from jax.experimental.pallas import tpu as pltpu
from jax.sharding import PartitionSpec as P

MESH = pl.DeviceIdType.MESH
NT = (((1,), (1,)), ((), ()))
NX, NY = 4, 4
MOST = 6
NONE = 2**30
TILE = 256


def far_first(sizes):
    steps = [(a, b) for a in range(sizes[0]) for b in range(sizes[1]) if a or b]
    return sorted(steps, key=lambda s: -sum(min(a, n - a) for a, n in zip(s, sizes)))


PLANE = far_first((NX, NY))


def place():
    group = lax.axis_index("group")
    return group // (2 * NY), (group // 2) % NY, group % 2, lax.axis_index("dev")


def device(x, y, c, z):
    return ((x * NY + y) * 2 + c, z)


def find_picks(chosen, position, rows):
    cands = chosen.shape[1]
    order = lax.broadcasted_iota(jnp.int32, chosen.shape, 1)
    within = chosen - position * rows
    owned = (within >= 0) & (within < rows)
    key = jnp.where(owned, within * cands + order, NONE)
    found = []
    for _ in range(MOST):
        least = jnp.min(key, axis=1, keepdims=True)
        key = jnp.where(key == least, NONE, key)
        index = jnp.minimum(least, rows * cands - 1) // cands
        tile = index // 16
        found.append((tile, index - tile * 16))
    return found


def picked_rows(found, emb_ref):
    line = lax.broadcasted_iota(jnp.int32, (16, emb_ref.shape[2]), 0)
    picked = []
    for turn in range(2):
        for tile, inside in found:
            block = emb_ref[tile[turn, 0]].astype(jnp.float32)
            here = line == inside[turn : turn + 1, :]
            picked.append(jnp.sum(jnp.where(here, block, 0.0), axis=0, keepdims=True) * -2.0)
    return jnp.concatenate(picked, axis=0)


def slot_sources(chosen_ref, x, y, z, rows, nz):
    cands = chosen_ref.shape[1]
    per = 2 * cands // nz
    turn = z // (nz // 2)
    start = (z % (nz // 2)) * per
    every = chosen_ref[0:1, :] * (1 - turn) + chosen_ref[1:2, :] * turn
    order = lax.broadcasted_iota(jnp.int32, (per, cands), 1)
    place_in = lax.broadcasted_iota(jnp.int32, (per, cands), 0) + start
    mine = jnp.sum(jnp.where(order == place_in, every, 0), axis=1, keepdims=True)
    owner = mine // rows
    earlier = (every < mine) | ((every == mine) & (order < place_in))
    rank = jnp.sum(jnp.where((every // rows == owner) & earlier, 1, 0), axis=1, keepdims=True)
    slot = turn * MOST + rank
    group = owner // nz
    source = ((owner - group * nz) * 2 + group % 2) * 16
    here = group // 2 == x * NY + y
    lane = lax.broadcasted_iota(jnp.int32, (per, 32 * nz), 1)
    main = (here & (lane == source + slot)).astype(jnp.bfloat16)
    low = here & (lane == source + 12 + slot % 4)
    tails = [(low & (slot // 4 == i)).astype(jnp.bfloat16) for i in range(3)]
    return main, tails


def kernel(
    chosen_hbm, near_hbm, emb_hbm, out_ref, cost_ref,
    chosen_ref, near_ref, emb, sent, col, parts, shares, ours, cand, least, sum_z, sum_xy,
    in_sem, zs, zr, ps, pr, os, orr, bs, cs, ks, slab_r, sib_r, azs, azr, axs, axr, total_rows,
):
    x, y, c, z = place()
    nz = lax.axis_size("dev")
    position = lax.axis_index("group") * nz + z
    rows = emb.shape[0] * 16
    slab = 4 * nz
    half = emb.shape[2] // 2
    cut = 3 * half // 4
    at_z, at_xy = z * 2 + c, x * NY + y
    major, minor = (y, x), (x, y)

    load = pltpu.make_async_copy(emb_hbm, emb, in_sem.at[0])
    load_chosen = pltpu.make_async_copy(chosen_hbm, chosen_ref, in_sem.at[1])
    load_near = pltpu.make_async_copy(near_hbm, near_ref, in_sem.at[2])
    load_chosen.start()
    load.start()
    load_near.start()

    column = [((z + dz) % nz, (c + dc) % 2) for dz, dc in far_first((nz, 2))]
    plane = [((x + dx) % NX, (y + dy) % NY) for dx, dy in PLANE]
    barrier = pltpu.get_barrier_semaphore()
    for tz, tc in column:
        pl.semaphore_signal(barrier, inc=1, device_id=device(x, y, tc, tz), device_id_type=MESH)
    for tx, ty in plane:
        pl.semaphore_signal(barrier, inc=1, device_id=device(tx, ty, c, z), device_id_type=MESH)

    least[...] = jnp.full(least.shape, jnp.inf, jnp.float32)
    load_chosen.wait()
    picks = find_picks(chosen_ref[...], position, rows)
    load.wait()
    found = picked_rows(picks, emb)
    for h in range(2):
        wide = found[:, half * h : half * (h + 1)]
        tail = jnp.concatenate([wide[4 * i : 4 * i + 4, cut:] for i in range(3)], axis=1)
        sent[h] = jnp.concatenate([wide[:, :cut], tail], axis=0).astype(jnp.bfloat16)
    col[at_z] = sent[c]
    pl.semaphore_wait(barrier, len(column) + len(plane))

    def remote(src, dst, ssem, rsem, target):
        return pltpu.make_async_remote_copy(
            src_ref=src, dst_ref=dst, send_sem=ssem, recv_sem=rsem,
            device_id=target, device_id_type=MESH)

    def slots_copy(i):
        tz, tc = column[i]
        return remote(sent.at[tc], col.at[at_z], zs.at[i], zr.at[at_z], device(x, y, tc, tz))

    def slots_arrival(i):
        tz, tc = column[i]
        t = tz * 2 + tc
        return remote(sent.at[tc], col.at[t], zs.at[i], zr.at[t], device(x, y, tc, tz))

    for i in range(len(column)):
        slots_copy(i).start()

    for j in range(rows // 128):
        part = emb[8 * j : 8 * (j + 1)].reshape(128, -1).astype(jnp.float32)
        part = part * part
        part = sum(part[:, 128 * i : 128 * (i + 1)] for i in range(part.shape[1] // 128))
        out_ref[:, 128 * j : 128 * (j + 1)] = jnp.sum(part.T, axis=0, keepdims=True)

    main, tails = slot_sources(chosen_ref, x, y, z, rows, nz)
    for i in range(len(column)):
        slots_arrival(i).wait_recv()

    gathered = col[...].reshape(-1, cut)
    left = jnp.dot(main, gathered, preferred_element_type=jnp.float32)
    right = sum(
        jnp.dot(tail, gathered[:, 128 * i : 128 * (i + 1)], preferred_element_type=jnp.float32)
        for i, tail in enumerate(tails)
    )
    dense = jnp.concatenate([left, right], axis=1)
    for t in range(NX * NY):
        rows8 = dense[8 * t : 8 * t + 8]
        both = jnp.concatenate([rows8[:, : half // 2], rows8[:, half // 2 :]], axis=0)
        parts[t] = both.astype(jnp.bfloat16)
    shares[at_xy] = parts[at_xy]

    def part_copy(i):
        tx, ty = plane[i]
        t = tx * NY + ty
        return remote(parts.at[t], shares.at[at_xy], ps.at[i], pr.at[at_xy], device(tx, ty, c, z))

    def part_arrival(i):
        tx, ty = plane[i]
        t = tx * NY + ty
        return remote(parts.at[t], shares.at[t], ps.at[i], pr.at[t], device(tx, ty, c, z))

    for i in range(len(plane)):
        part_copy(i).start()
    for i in range(len(plane)):
        part_arrival(i).wait_recv()
    ours[z] = jnp.sum(shares[...].astype(jnp.float32), axis=0).astype(jnp.bfloat16)

    def z_copy(k):
        return remote(ours.at[z], ours.at[z], os.at[k - 1], orr.at[z], device(x, y, c, (z + k) % nz))

    def z_arrival(k):
        t = (z + k) % nz
        return remote(ours.at[t], ours.at[t], os.at[k - 1], orr.at[t], device(x, y, c, t))

    for k in (4, 3, 5, 2, 6, 1, 7):
        z_copy(k).start()
    for k in range(1, nz):
        z_arrival(k).wait_recv()
    for p in range(2):
        rows8 = [ours[p * (nz // 2) + t].astype(jnp.float32) for t in range(nz // 2)]
        packed = [jnp.concatenate([r[:8], r[8:]], axis=1) for r in rows8]
        start = pl.multiple_of(minor[p] * slab, 16)
        cand[p, c, major[p], pl.ds(start, slab), :] = jnp.concatenate(packed, axis=0).astype(
            jnp.bfloat16
        )

    def slab_at(p, a, b, core):
        start = pl.multiple_of(b * slab, 16)
        return cand.at[p, core, a, pl.ds(start, slab), :]

    def spot(p, a, b):
        return (b, a) if p == 0 else (a, b)

    def copy(p, a, b, core, ssem, rsem, target):
        ref = slab_at(p, a, b, core)
        return remote(ref, ref, ssem, rsem, target)

    def major_copy(p, k):
        a, b = major[p], minor[p]
        tx, ty = spot(p, (a + k) % 4, b)
        return copy(p, a, b, c, bs.at[p, k - 1], slab_r.at[p, a, b], device(tx, ty, c, z))

    def minor_copy(p, a, k):
        b = minor[p]
        tx, ty = spot(p, major[p], (b + k) % 4)
        return copy(p, a, b, c, cs.at[p, a, k - 1], slab_r.at[p, a, b], device(tx, ty, c, z))

    def core_copy(p, a, b):
        return copy(p, a, b, c, ks.at[p, a, b], sib_r.at[p, a, b], device(x, y, 1 - c, z))

    def slab_arrival(p, a, b):
        return copy(p, a, b, c, ks.at[p, a, b], slab_r.at[p, a, b], device(x, y, 1 - c, z))

    def core_arrival(p, a, b):
        return copy(p, a, b, 1 - c, ks.at[p, a, b], sib_r.at[p, a, b], device(x, y, 1 - c, z))

    for k in (2, 1, 3):
        for p in range(2):
            major_copy(p, k).start()
    for p in range(2):
        for k in (2, 1, 3):
            minor_copy(p, major[p], k).start()
        core_copy(p, major[p], minor[p]).start()
    for k in (1, 3, 2):
        for p in range(2):
            a = (major[p] + k) % 4
            slab_arrival(p, a, minor[p]).wait_recv()
            for j in (2, 1, 3):
                minor_copy(p, a, j).start()
            core_copy(p, a, minor[p]).start()

    def pass_on(p, k):
        a = (major[p] + k) % 4
        for j in (1, 3, 2):
            b = (minor[p] + j) % 4
            slab_arrival(p, a, b).wait_recv()
            core_copy(p, a, b).start()

    def absorb(k):
        at = [(major[p] + k) % 4 for p in range(2)]
        for p in range(2):
            for b in range(4):
                core_arrival(p, at[p], b).wait_recv()
        blocks = [jnp.concatenate([cand[p, h, at[p]] for p in range(2)], axis=0) for h in range(2)]
        wide = [block.astype(jnp.float32) for block in blocks]
        norm = jnp.sum(wide[0] * wide[0] + wide[1] * wide[1], axis=1, keepdims=True) * 0.25
        for j in range(rows // TILE):
            lanes = slice(TILE * j, TILE * (j + 1))
            mine = emb[TILE // 16 * j : TILE // 16 * (j + 1)].reshape(TILE, -1)
            product = sum(
                lax.dot_general(
                    blocks[h], mine[:, half * h : half * (h + 1)], NT,
                    preferred_element_type=jnp.float32)
                for h in range(2)
            )
            reach = jnp.min((product + norm).reshape(2, -1, 8, TILE), axis=1)
            least[:, :, lanes] = jnp.minimum(least[:, :, lanes], reach)

    def pass_both(k):
        for p in range(2):
            pass_on(p, k)

    pass_both(0)
    absorb(0)
    pass_both(1)
    pass_both(3)
    absorb(1)
    pass_both(2)
    absorb(3)
    absorb(2)
    load_near.wait()

    norms = out_ref[...]
    near = near_ref[...]
    sums = []
    for p in range(2):
        reach = jnp.min(least[p], axis=0, keepdims=True)
        near = jnp.minimum(near, jnp.maximum(norms + reach, 0.0))
        sums.append(jnp.sum(near, axis=1, keepdims=True))
    lane = lax.broadcasted_iota(jnp.int32, (1, 128), 1)
    share = jnp.where(lane == 0, sums[0], jnp.where(lane == 1, sums[1], 0.0))

    sum_z[at_z] = share
    for i, (tz, tc) in enumerate(column):
        pltpu.make_async_remote_copy(
            src_ref=sum_z.at[at_z], dst_ref=sum_z.at[at_z], send_sem=azs.at[i],
            recv_sem=azr.at[at_z], device_id=device(x, y, tc, tz), device_id_type=MESH).start()
    out_ref[...] = near
    for i, (tz, tc) in enumerate(column):
        t = tz * 2 + tc
        pltpu.make_async_remote_copy(
            src_ref=sum_z.at[t], dst_ref=sum_z.at[t], send_sem=azs.at[i],
            recv_sem=azr.at[t], device_id=device(x, y, tc, tz), device_id_type=MESH).wait_recv()
    sum_xy[at_xy] = jnp.sum(sum_z[...], axis=0)
    for i, (tx, ty) in enumerate(plane):
        pltpu.make_async_remote_copy(
            src_ref=sum_xy.at[at_xy], dst_ref=sum_xy.at[at_xy], send_sem=axs.at[i],
            recv_sem=axr.at[at_xy], device_id=device(tx, ty, c, z), device_id_type=MESH).start()

    for i in range(len(column)):
        slots_copy(i).wait_send()
    for i in range(len(plane)):
        part_copy(i).wait_send()
    for k in range(1, nz):
        z_copy(k).wait_send()
    for p in range(2):
        for k in (1, 2, 3):
            major_copy(p, k).wait_send()
        for a in range(4):
            for k in (1, 2, 3):
                minor_copy(p, a, k).wait_send()
            for b in range(4):
                core_copy(p, a, b).wait_send()
    for i, (tz, tc) in enumerate(column):
        pltpu.make_async_remote_copy(
            src_ref=sum_z.at[at_z], dst_ref=sum_z.at[at_z], send_sem=azs.at[i],
            recv_sem=azr.at[at_z], device_id=device(x, y, tc, tz), device_id_type=MESH).wait_send()

    for i, (tx, ty) in enumerate(plane):
        t = tx * NY + ty
        both = pltpu.make_async_remote_copy(
            src_ref=sum_xy.at[t], dst_ref=sum_xy.at[t], send_sem=axs.at[i],
            recv_sem=axr.at[t], device_id=device(tx, ty, c, z), device_id_type=MESH)
        both.wait_recv()
        both.wait_send()
    final = jnp.sum(sum_xy[...], axis=0) / total_rows
    cost_ref[0] = final[0, 0]
    cost_ref[1] = final[0, 1]


def local(embeddings, nearest, chosen):
    rows, width = embeddings.shape
    nz = lax.axis_size("dev")
    total_rows = rows * nz * lax.axis_size("group")
    dma = pltpu.SemaphoreType.DMA

    near, cost = pl.pallas_call(
        functools.partial(kernel, total_rows=total_rows),
        out_shape=(
            jax.ShapeDtypeStruct((1, rows), jnp.float32),
            jax.ShapeDtypeStruct((2,), jnp.float32),
        ),
        in_specs=[
            pl.BlockSpec(memory_space=pl.ANY),
            pl.BlockSpec(memory_space=pl.ANY),
            pl.BlockSpec(memory_space=pl.ANY),
        ],
        out_specs=(
            pl.BlockSpec(memory_space=pltpu.VMEM),
            pl.BlockSpec(memory_space=pltpu.SMEM),
        ),
        scratch_shapes=[
            pltpu.VMEM(chosen.shape, jnp.int32),
            pltpu.VMEM((1, rows), jnp.float32),
            pltpu.VMEM((rows // 16, 16, width), jnp.bfloat16),
            pltpu.VMEM((2, 16, 3 * width // 8), jnp.bfloat16),
            pltpu.VMEM((2 * nz, 16, 3 * width // 8), jnp.bfloat16),
            pltpu.VMEM((NX * NY, 16, width // 4), jnp.bfloat16),
            pltpu.VMEM((NX * NY, 16, width // 4), jnp.bfloat16),
            pltpu.VMEM((nz, 16, width // 4), jnp.bfloat16),
            pltpu.VMEM((2, 2, 4, 16 * nz, width // 2), jnp.bfloat16),
            pltpu.VMEM((2, 8, rows), jnp.float32),
            pltpu.VMEM((2 * nz, 1, 128), jnp.float32),
            pltpu.VMEM((NX * NY, 1, 128), jnp.float32),
            dma((3,)),
            dma((2 * nz - 1,)),
            dma((2 * nz,)),
            dma((NX * NY - 1,)),
            dma((NX * NY,)),
            dma((nz - 1,)),
            dma((nz,)),
            dma((2, 3)),
            dma((2, 4, 3)),
            dma((2, 4, 4)),
            dma((2, 4, 4)),
            dma((2, 4, 4)),
            dma((2 * nz - 1,)),
            dma((2 * nz,)),
            dma((NX * NY - 1,)),
            dma((NX * NY,)),
        ],
        compiler_params=pltpu.CompilerParams(
            collective_id=0, has_side_effects=True, vmem_limit_bytes=60 * 2**20
        ),
        cost_estimate=pl.CostEstimate(
            flops=4 * rows * width * chosen.shape[1], bytes_accessed=rows * width * 2, transcendentals=0
        ),
    )(chosen, nearest.reshape(1, rows), embeddings.reshape(rows // 16, 16, width))
    return near.reshape(rows), cost


def solution(mesh):
    return jax.shard_map(
        local,
        mesh=mesh,
        in_specs=(P(("group", "dev"), None), P(("group", "dev")), P()),
        out_specs=(P(("group", "dev")), P()),
        check_vma=False,
    )
```

```python
import functools

import jax
import jax.numpy as jnp
from jax import lax
from jax.experimental import pallas as pl
from jax.experimental.pallas import tpu as pltpu
from jax.sharding import PartitionSpec as P

MESH = pl.DeviceIdType.MESH
NT = (((1,), (1,)), ((), ()))
NX, NY = 4, 4
MOST = 6
NONE = 2**30
TILE = 256


def far_first(sizes):
    steps = [(a, b) for a in range(sizes[0]) for b in range(sizes[1]) if a or b]
    return sorted(steps, key=lambda s: -sum(min(a, n - a) for a, n in zip(s, sizes)))


PLANE = far_first((NX, NY))


def place():
    group = lax.axis_index("group")
    return group // (2 * NY), (group // 2) % NY, group % 2, lax.axis_index("dev")


def device(x, y, c, z):
    return ((x * NY + y) * 2 + c, z)


def find_picks(chosen, position, rows):
    cands = chosen.shape[1]
    order = lax.broadcasted_iota(jnp.int32, chosen.shape, 1)
    within = chosen - position * rows
    owned = (within >= 0) & (within < rows)
    key = jnp.where(owned, within * cands + order, NONE)
    found = []
    for _ in range(MOST):
        least = jnp.min(key, axis=1, keepdims=True)
        key = jnp.where(key == least, NONE, key)
        index = jnp.minimum(least, rows * cands - 1) // cands
        tile = index // 16
        found.append((tile, index - tile * 16))
    return found


def picked_rows(found, emb_ref):
    line = lax.broadcasted_iota(jnp.int32, (16, emb_ref.shape[2]), 0)
    picked = []
    for turn in range(2):
        for tile, inside in found:
            block = emb_ref[tile[turn, 0]].astype(jnp.float32)
            here = line == inside[turn : turn + 1, :]
            picked.append(jnp.sum(jnp.where(here, block, 0.0), axis=0, keepdims=True) * -2.0)
    return jnp.concatenate(picked, axis=0)


def slot_sources(chosen_ref, x, y, z, rows, nz):
    cands = chosen_ref.shape[1]
    per = 2 * cands // nz
    turn = z // (nz // 2)
    start = (z % (nz // 2)) * per
    every = chosen_ref[0:1, :] * (1 - turn) + chosen_ref[1:2, :] * turn
    order = lax.broadcasted_iota(jnp.int32, (per, cands), 1)
    place_in = lax.broadcasted_iota(jnp.int32, (per, cands), 0) + start
    mine = jnp.sum(jnp.where(order == place_in, every, 0), axis=1, keepdims=True)
    owner = mine // rows
    earlier = (every < mine) | ((every == mine) & (order < place_in))
    rank = jnp.sum(jnp.where((every // rows == owner) & earlier, 1, 0), axis=1, keepdims=True)
    slot = turn * MOST + rank
    group = owner // nz
    source = ((owner - group * nz) * 2 + group % 2) * 16
    here = group // 2 == x * NY + y
    lane = lax.broadcasted_iota(jnp.int32, (per, 32 * nz), 1)
    main = (here & (lane == source + slot)).astype(jnp.bfloat16)
    low = here & (lane == source + 12 + slot % 4)
    tails = [(low & (slot // 4 == i)).astype(jnp.bfloat16) for i in range(3)]
    return main, tails


def kernel(
    chosen_hbm, near_hbm, emb_hbm, result,
    out_ref, chosen_ref, near_ref, emb, sent, col, parts, shares, ours, cand, least, sum_z, sum_xy,
    in_sem, zs, zr, ps, pr, os, orr, bs, cs, ks, slab_r, sib_r, azs, azr, axs, axr, total_rows,
):
    x, y, c, z = place()
    nz = lax.axis_size("dev")
    position = lax.axis_index("group") * nz + z
    rows = emb.shape[0] * 16
    slab = 4 * nz
    half = emb.shape[2] // 2
    cut = 3 * half // 4
    at_z, at_xy = z * 2 + c, x * NY + y
    major, minor = (y, x), (x, y)

    load = pltpu.make_async_copy(emb_hbm, emb, in_sem.at[0])
    load_chosen = pltpu.make_async_copy(chosen_hbm, chosen_ref, in_sem.at[1])
    load_near = pltpu.make_async_copy(near_hbm, near_ref, in_sem.at[2])
    load_chosen.start()
    load.start()
    load_near.start()

    column = [((z + dz) % nz, (c + dc) % 2) for dz, dc in far_first((nz, 2))]
    plane = [((x + dx) % NX, (y + dy) % NY) for dx, dy in PLANE]
    barrier = pltpu.get_barrier_semaphore()
    for tz, tc in column:
        pl.semaphore_signal(barrier, inc=1, device_id=device(x, y, tc, tz), device_id_type=MESH)
    for tx, ty in plane:
        pl.semaphore_signal(barrier, inc=1, device_id=device(tx, ty, c, z), device_id_type=MESH)

    least[...] = jnp.full(least.shape, jnp.inf, jnp.float32)
    load_chosen.wait()
    picks = find_picks(chosen_ref[...], position, rows)
    load.wait()
    found = picked_rows(picks, emb)
    for h in range(2):
        wide = found[:, half * h : half * (h + 1)]
        tail = jnp.concatenate([wide[4 * i : 4 * i + 4, cut:] for i in range(3)], axis=1)
        sent[h] = jnp.concatenate([wide[:, :cut], tail], axis=0).astype(jnp.bfloat16)
    col[at_z] = sent[c]
    pl.semaphore_wait(barrier, len(column) + len(plane))

    def remote(src, dst, ssem, rsem, target):
        return pltpu.make_async_remote_copy(
            src_ref=src, dst_ref=dst, send_sem=ssem, recv_sem=rsem,
            device_id=target, device_id_type=MESH)

    def slots_copy(i):
        tz, tc = column[i]
        return remote(sent.at[tc], col.at[at_z], zs.at[i], zr.at[at_z], device(x, y, tc, tz))

    def slots_arrival(i):
        tz, tc = column[i]
        t = tz * 2 + tc
        return remote(sent.at[tc], col.at[t], zs.at[i], zr.at[t], device(x, y, tc, tz))

    for i in range(len(column)):
        slots_copy(i).start()

    for j in range(rows // 128):
        part = emb[8 * j : 8 * (j + 1)].reshape(128, -1).astype(jnp.float32)
        part = part * part
        part = sum(part[:, 128 * i : 128 * (i + 1)] for i in range(part.shape[1] // 128))
        out_ref[:, 128 * j : 128 * (j + 1)] = jnp.sum(part.T, axis=0, keepdims=True)

    main, tails = slot_sources(chosen_ref, x, y, z, rows, nz)
    for i in range(len(column)):
        slots_arrival(i).wait_recv()

    gathered = col[...].reshape(-1, cut)
    left = jnp.dot(main, gathered, preferred_element_type=jnp.float32)
    right = sum(
        jnp.dot(tail, gathered[:, 128 * i : 128 * (i + 1)], preferred_element_type=jnp.float32)
        for i, tail in enumerate(tails)
    )
    dense = jnp.concatenate([left, right], axis=1)
    for t in range(NX * NY):
        rows8 = dense[8 * t : 8 * t + 8]
        both = jnp.concatenate([rows8[:, : half // 2], rows8[:, half // 2 :]], axis=0)
        parts[t] = both.astype(jnp.bfloat16)
    shares[at_xy] = parts[at_xy]

    def part_copy(i):
        tx, ty = plane[i]
        t = tx * NY + ty
        return remote(parts.at[t], shares.at[at_xy], ps.at[i], pr.at[at_xy], device(tx, ty, c, z))

    def part_arrival(i):
        tx, ty = plane[i]
        t = tx * NY + ty
        return remote(parts.at[t], shares.at[t], ps.at[i], pr.at[t], device(tx, ty, c, z))

    for i in range(len(plane)):
        part_copy(i).start()
    for i in range(len(plane)):
        part_arrival(i).wait_recv()
    ours[z] = jnp.sum(shares[...].astype(jnp.float32), axis=0).astype(jnp.bfloat16)

    def z_copy(k):
        return remote(ours.at[z], ours.at[z], os.at[k - 1], orr.at[z], device(x, y, c, (z + k) % nz))

    def z_arrival(k):
        t = (z + k) % nz
        return remote(ours.at[t], ours.at[t], os.at[k - 1], orr.at[t], device(x, y, c, t))

    for k in (4, 3, 5, 2, 6, 1, 7):
        z_copy(k).start()
    for k in range(1, nz):
        z_arrival(k).wait_recv()
    for p in range(2):
        rows8 = [ours[p * (nz // 2) + t].astype(jnp.float32) for t in range(nz // 2)]
        packed = [jnp.concatenate([r[:8], r[8:]], axis=1) for r in rows8]
        start = pl.multiple_of(minor[p] * slab, 16)
        cand[p, c, major[p], pl.ds(start, slab), :] = jnp.concatenate(packed, axis=0).astype(
            jnp.bfloat16
        )

    def slab_at(p, a, b, core):
        start = pl.multiple_of(b * slab, 16)
        return cand.at[p, core, a, pl.ds(start, slab), :]

    def spot(p, a, b):
        return (b, a) if p == 0 else (a, b)

    def copy(p, a, b, core, ssem, rsem, target):
        ref = slab_at(p, a, b, core)
        return remote(ref, ref, ssem, rsem, target)

    def major_copy(p, k):
        a, b = major[p], minor[p]
        tx, ty = spot(p, (a + k) % 4, b)
        return copy(p, a, b, c, bs.at[p, k - 1], slab_r.at[p, a, b], device(tx, ty, c, z))

    def minor_copy(p, a, k):
        b = minor[p]
        tx, ty = spot(p, major[p], (b + k) % 4)
        return copy(p, a, b, c, cs.at[p, a, k - 1], slab_r.at[p, a, b], device(tx, ty, c, z))

    def core_copy(p, a):
        ref = cand.at[p, c, a]
        return remote(ref, ref, ks.at[p, a], sib_r.at[p, a], device(x, y, 1 - c, z))

    def slab_arrival(p, a, b):
        return copy(p, a, b, c, ks.at[p, a], slab_r.at[p, a, b], device(x, y, 1 - c, z))

    def core_arrival(p, a):
        ref = cand.at[p, 1 - c, a]
        return remote(ref, ref, ks.at[p, a], sib_r.at[p, a], device(x, y, 1 - c, z))

    for k in (2, 1, 3):
        for p in range(2):
            major_copy(p, k).start()
    for p in range(2):
        for k in (2, 1, 3):
            minor_copy(p, major[p], k).start()
    for k in (1, 3, 2):
        for p in range(2):
            a = (major[p] + k) % 4
            slab_arrival(p, a, minor[p]).wait_recv()
            for j in (2, 1, 3):
                minor_copy(p, a, j).start()

    def pass_on(p, k):
        a = (major[p] + k) % 4
        for j in (1, 3, 2):
            b = (minor[p] + j) % 4
            slab_arrival(p, a, b).wait_recv()
        core_copy(p, a).start()

    def absorb(k):
        at = [(major[p] + k) % 4 for p in range(2)]
        for p in range(2):
            core_arrival(p, at[p]).wait_recv()
        blocks = [jnp.concatenate([cand[p, h, at[p]] for p in range(2)], axis=0) for h in range(2)]
        wide = [block.astype(jnp.float32) for block in blocks]
        norm = jnp.sum(wide[0] * wide[0] + wide[1] * wide[1], axis=1, keepdims=True) * 0.25
        for j in range(rows // TILE):
            lanes = slice(TILE * j, TILE * (j + 1))
            mine = emb[TILE // 16 * j : TILE // 16 * (j + 1)].reshape(TILE, -1)
            product = sum(
                lax.dot_general(
                    blocks[h], mine[:, half * h : half * (h + 1)], NT,
                    preferred_element_type=jnp.float32)
                for h in range(2)
            )
            reach = jnp.min((product + norm).reshape(2, -1, 8, TILE), axis=1)
            least[:, :, lanes] = jnp.minimum(least[:, :, lanes], reach)

    def pass_both(k):
        for p in range(2):
            pass_on(p, k)

    pass_both(0)
    absorb(0)
    pass_both(1)
    pass_both(3)
    absorb(1)
    pass_both(2)
    absorb(3)
    absorb(2)
    load_near.wait()

    norms = out_ref[...]
    near = near_ref[...]
    sums = []
    for p in range(2):
        reach = jnp.min(least[p], axis=0, keepdims=True)
        near = jnp.minimum(near, jnp.maximum(norms + reach, 0.0))
        sums.append(jnp.sum(near, axis=1, keepdims=True))
    lane = lax.broadcasted_iota(jnp.int32, (1, 128), 1)
    share = jnp.where(lane == 0, sums[0], jnp.where(lane == 1, sums[1], 0.0))

    sum_z[at_z] = share
    for i, (tz, tc) in enumerate(column):
        pltpu.make_async_remote_copy(
            src_ref=sum_z.at[at_z], dst_ref=sum_z.at[at_z], send_sem=azs.at[i],
            recv_sem=azr.at[at_z], device_id=device(x, y, tc, tz), device_id_type=MESH).start()
    out_ref[...] = near
    store = pltpu.make_async_copy(out_ref, result.at[:, pl.ds(0, rows)], in_sem.at[0])
    store.start()
    for i, (tz, tc) in enumerate(column):
        t = tz * 2 + tc
        pltpu.make_async_remote_copy(
            src_ref=sum_z.at[t], dst_ref=sum_z.at[t], send_sem=azs.at[i],
            recv_sem=azr.at[t], device_id=device(x, y, tc, tz), device_id_type=MESH).wait_recv()
    sum_xy[at_xy] = jnp.sum(sum_z[...], axis=0)
    for i, (tx, ty) in enumerate(plane):
        pltpu.make_async_remote_copy(
            src_ref=sum_xy.at[at_xy], dst_ref=sum_xy.at[at_xy], send_sem=axs.at[i],
            recv_sem=axr.at[at_xy], device_id=device(tx, ty, c, z), device_id_type=MESH).start()

    for i in range(len(column)):
        slots_copy(i).wait_send()
    for i in range(len(plane)):
        part_copy(i).wait_send()
    for k in range(1, nz):
        z_copy(k).wait_send()
    for p in range(2):
        for k in (1, 2, 3):
            major_copy(p, k).wait_send()
        for a in range(4):
            for k in (1, 2, 3):
                minor_copy(p, a, k).wait_send()
            core_copy(p, a).wait_send()
    for i, (tz, tc) in enumerate(column):
        pltpu.make_async_remote_copy(
            src_ref=sum_z.at[at_z], dst_ref=sum_z.at[at_z], send_sem=azs.at[i],
            recv_sem=azr.at[at_z], device_id=device(x, y, tc, tz), device_id_type=MESH).wait_send()

    for i, (tx, ty) in enumerate(plane):
        t = tx * NY + ty
        both = pltpu.make_async_remote_copy(
            src_ref=sum_xy.at[t], dst_ref=sum_xy.at[t], send_sem=axs.at[i],
            recv_sem=axr.at[t], device_id=device(tx, ty, c, z), device_id_type=MESH)
        both.wait_recv()
        both.wait_send()
    sum_xy[0] = jnp.sum(sum_xy[...], axis=0) / total_rows
    last = pltpu.make_async_copy(sum_xy.at[0], result.at[:, pl.ds(rows, 128)], in_sem.at[1])
    last.start()
    store.wait()
    last.wait()


def finish(result, near_out, cost_out):
    rows = near_out.shape[1]
    near_out[...] = result[:, :rows]
    cost_out[0] = result[0, rows]
    cost_out[1] = result[0, rows + 1]


def local(embeddings, nearest, chosen):
    rows, width = embeddings.shape
    nz = lax.axis_size("dev")
    total_rows = rows * nz * lax.axis_size("group")
    dma = pltpu.SemaphoreType.DMA

    result = pl.pallas_call(
        functools.partial(kernel, total_rows=total_rows),
        out_shape=jax.ShapeDtypeStruct((1, rows + 128), jnp.float32),
        in_specs=[
            pl.BlockSpec(memory_space=pl.ANY),
            pl.BlockSpec(memory_space=pl.ANY),
            pl.BlockSpec(memory_space=pl.ANY),
        ],
        out_specs=pl.BlockSpec(memory_space=pl.ANY),
        scratch_shapes=[
            pltpu.VMEM((1, rows), jnp.float32),
            pltpu.VMEM(chosen.shape, jnp.int32),
            pltpu.VMEM((1, rows), jnp.float32),
            pltpu.VMEM((rows // 16, 16, width), jnp.bfloat16),
            pltpu.VMEM((2, 16, 3 * width // 8), jnp.bfloat16),
            pltpu.VMEM((2 * nz, 16, 3 * width // 8), jnp.bfloat16),
            pltpu.VMEM((NX * NY, 16, width // 4), jnp.bfloat16),
            pltpu.VMEM((NX * NY, 16, width // 4), jnp.bfloat16),
            pltpu.VMEM((nz, 16, width // 4), jnp.bfloat16),
            pltpu.VMEM((2, 2, 4, 16 * nz, width // 2), jnp.bfloat16),
            pltpu.VMEM((2, 8, rows), jnp.float32),
            pltpu.VMEM((2 * nz, 1, 128), jnp.float32),
            pltpu.VMEM((NX * NY, 1, 128), jnp.float32),
            dma((3,)),
            dma((2 * nz - 1,)),
            dma((2 * nz,)),
            dma((NX * NY - 1,)),
            dma((NX * NY,)),
            dma((nz - 1,)),
            dma((nz,)),
            dma((2, 3)),
            dma((2, 4, 3)),
            dma((2, 4)),
            dma((2, 4, 4)),
            dma((2, 4)),
            dma((2 * nz - 1,)),
            dma((2 * nz,)),
            dma((NX * NY - 1,)),
            dma((NX * NY,)),
        ],
        compiler_params=pltpu.CompilerParams(
            collective_id=0, has_side_effects=True, vmem_limit_bytes=60 * 2**20
        ),
        cost_estimate=pl.CostEstimate(
            flops=4 * rows * width * chosen.shape[1], bytes_accessed=rows * width * 2, transcendentals=0
        ),
    )(chosen, nearest.reshape(1, rows), embeddings.reshape(rows // 16, 16, width))
    near, cost = pl.pallas_call(
        finish,
        out_shape=(
            jax.ShapeDtypeStruct((1, rows), jnp.float32),
            jax.ShapeDtypeStruct((2,), jnp.float32),
        ),
        in_specs=[
            pl.BlockSpec(memory_space=pltpu.VMEM),
        ],
        out_specs=(
            pl.BlockSpec(memory_space=pltpu.VMEM),
            pl.BlockSpec(memory_space=pltpu.SMEM),
        ),
        compiler_params=pltpu.CompilerParams(vmem_limit_bytes=60 * 2**20),
    )(result)
    return near.reshape(rows), cost


def solution(mesh):
    return jax.shard_map(
        local,
        mesh=mesh,
        in_specs=(P(("group", "dev"), None), P(("group", "dev")), P()),
        out_specs=(P(("group", "dev")), P()),
        check_vma=False,
    )
```

```python
import functools
import itertools

import jax
import jax.numpy as jnp
from jax import lax
from jax.experimental import pallas as pl
from jax.experimental.pallas import tpu as pltpu
from jax.sharding import PartitionSpec as P

MESH = pl.DeviceIdType.MESH
NT = (((1,), (1,)), ((), ()))
NX, NY = 4, 4
MOST = 6
NONE = 2**30
TILE = 256


def far_first(sizes):
    steps = [s for s in itertools.product(*map(range, sizes)) if any(s)]
    return sorted(steps, key=lambda s: -sum(min(a, n - a) for a, n in zip(s, sizes)))


PLANE = far_first((NX, NY))


def place():
    group = lax.axis_index("group")
    return group // (2 * NY), (group // 2) % NY, group % 2, lax.axis_index("dev")


def device(x, y, c, z):
    return ((x * NY + y) * 2 + c, z)


def find_picks(chosen, position, rows):
    cands = chosen.shape[1]
    order = lax.broadcasted_iota(jnp.int32, chosen.shape, 1)
    within = chosen - position * rows
    owned = (within >= 0) & (within < rows)
    key = jnp.where(owned, within * cands + order, NONE)
    found = []
    for _ in range(MOST):
        least = jnp.min(key, axis=1, keepdims=True)
        key = jnp.where(key == least, NONE, key)
        index = jnp.minimum(least, rows * cands - 1) // cands
        tile = index // 16
        found.append((tile, index - tile * 16))
    return found


def picked_rows(found, emb_ref):
    line = lax.broadcasted_iota(jnp.int32, (16, emb_ref.shape[2]), 0)
    picked = []
    for turn in range(2):
        for tile, inside in found:
            block = emb_ref[tile[turn, 0]].astype(jnp.float32)
            here = line == inside[turn : turn + 1, :]
            picked.append(jnp.sum(jnp.where(here, block, 0.0), axis=0, keepdims=True) * -2.0)
    return jnp.concatenate(picked, axis=0)


def slot_sources(chosen_ref, x, y, z, rows, nz):
    cands = chosen_ref.shape[1]
    per = 2 * cands // nz
    turn = z // (nz // 2)
    start = (z % (nz // 2)) * per
    every = chosen_ref[0:1, :] * (1 - turn) + chosen_ref[1:2, :] * turn
    order = lax.broadcasted_iota(jnp.int32, (per, cands), 1)
    place_in = lax.broadcasted_iota(jnp.int32, (per, cands), 0) + start
    mine = jnp.sum(jnp.where(order == place_in, every, 0), axis=1, keepdims=True)
    owner = mine // rows
    earlier = (every < mine) | ((every == mine) & (order < place_in))
    rank = jnp.sum(jnp.where((every // rows == owner) & earlier, 1, 0), axis=1, keepdims=True)
    slot = turn * MOST + rank
    group = owner // nz
    source = ((owner - group * nz) * 2 + group % 2) * 16
    here = group // 2 == x * NY + y
    lane = lax.broadcasted_iota(jnp.int32, (per, 32 * nz), 1)
    main = (here & (lane == source + slot)).astype(jnp.bfloat16)
    low = here & (lane == source + 12 + slot % 4)
    tails = [(low & (slot // 4 == i)).astype(jnp.bfloat16) for i in range(3)]
    return main, tails


def kernel(
    chosen_hbm, near_hbm, emb_hbm, result,
    out_ref, chosen_ref, near_ref, emb, sent, col, parts, shares, ours, cand, least, sums_at, total,
    in_sem, zs, zr, ps, pr, os, orr, bs, cs, ks, slab_r, sib_r, sum_sem, total_rows,
):
    x, y, c, z = place()
    nz = lax.axis_size("dev")
    position = lax.axis_index("group") * nz + z
    rows = emb.shape[0] * 16
    slab = 4 * nz
    half = emb.shape[2] // 2
    cut = 3 * half // 4
    at_z, at_xy = z * 2 + c, x * NY + y
    major, minor = (y, x), (x, y)

    load = pltpu.make_async_copy(emb_hbm, emb, in_sem.at[0])
    load_chosen = pltpu.make_async_copy(chosen_hbm, chosen_ref, in_sem.at[1])
    load_near = pltpu.make_async_copy(near_hbm, near_ref, in_sem.at[2])
    load_chosen.start()
    load.start()
    load_near.start()

    column = [((z + dz) % nz, (c + dc) % 2) for dz, dc in far_first((nz, 2))]
    plane = [((x + dx) % NX, (y + dy) % NY) for dx, dy in PLANE]
    barrier = pltpu.get_barrier_semaphore()
    for tz, tc in column:
        pl.semaphore_signal(barrier, inc=1, device_id=device(x, y, tc, tz), device_id_type=MESH)
    for tx, ty in plane:
        pl.semaphore_signal(barrier, inc=1, device_id=device(tx, ty, c, z), device_id_type=MESH)

    least[...] = jnp.full(least.shape, jnp.inf, jnp.float32)
    load_chosen.wait()
    picks = find_picks(chosen_ref[...], position, rows)
    load.wait()
    found = picked_rows(picks, emb)
    for h in range(2):
        wide = found[:, half * h : half * (h + 1)]
        tail = jnp.concatenate([wide[4 * i : 4 * i + 4, cut:] for i in range(3)], axis=1)
        sent[h] = jnp.concatenate([wide[:, :cut], tail], axis=0).astype(jnp.bfloat16)
    col[at_z] = sent[c]
    pl.semaphore_wait(barrier, len(column) + len(plane))

    def remote(src, dst, ssem, rsem, target):
        return pltpu.make_async_remote_copy(
            src_ref=src, dst_ref=dst, send_sem=ssem, recv_sem=rsem,
            device_id=target, device_id_type=MESH)

    def slots_copy(i):
        tz, tc = column[i]
        return remote(sent.at[tc], col.at[at_z], zs.at[i], zr.at[at_z], device(x, y, tc, tz))

    def slots_arrival(i):
        tz, tc = column[i]
        t = tz * 2 + tc
        return remote(sent.at[tc], col.at[t], zs.at[i], zr.at[t], device(x, y, tc, tz))

    for i in range(len(column)):
        slots_copy(i).start()

    for j in range(rows // 128):
        part = emb[8 * j : 8 * (j + 1)].reshape(128, -1).astype(jnp.float32)
        part = part * part
        part = sum(part[:, 128 * i : 128 * (i + 1)] for i in range(part.shape[1] // 128))
        out_ref[:, 128 * j : 128 * (j + 1)] = jnp.sum(part.T, axis=0, keepdims=True)

    main, tails = slot_sources(chosen_ref, x, y, z, rows, nz)
    for i in range(len(column)):
        slots_arrival(i).wait_recv()

    gathered = col[...].reshape(-1, cut)
    left = jnp.dot(main, gathered, preferred_element_type=jnp.float32)
    right = sum(
        jnp.dot(tail, gathered[:, 128 * i : 128 * (i + 1)], preferred_element_type=jnp.float32)
        for i, tail in enumerate(tails)
    )
    dense = jnp.concatenate([left, right], axis=1)
    for t in range(NX * NY):
        rows8 = dense[8 * t : 8 * t + 8]
        both = jnp.concatenate([rows8[:, : half // 2], rows8[:, half // 2 :]], axis=0)
        parts[t] = both.astype(jnp.bfloat16)
    shares[at_xy] = parts[at_xy]

    def part_copy(i):
        tx, ty = plane[i]
        t = tx * NY + ty
        return remote(parts.at[t], shares.at[at_xy], ps.at[i], pr.at[at_xy], device(tx, ty, c, z))

    def part_arrival(i):
        tx, ty = plane[i]
        t = tx * NY + ty
        return remote(parts.at[t], shares.at[t], ps.at[i], pr.at[t], device(tx, ty, c, z))

    for i in range(len(plane)):
        part_copy(i).start()
    for i in range(len(plane)):
        part_arrival(i).wait_recv()
    ours[z] = jnp.sum(shares[...].astype(jnp.float32), axis=0).astype(jnp.bfloat16)

    def z_copy(k):
        return remote(ours.at[z], ours.at[z], os.at[k - 1], orr.at[z], device(x, y, c, (z + k) % nz))

    def z_arrival(k):
        t = (z + k) % nz
        return remote(ours.at[t], ours.at[t], os.at[k - 1], orr.at[t], device(x, y, c, t))

    for k in (4, 3, 5, 2, 6, 1, 7):
        z_copy(k).start()
    for k in range(1, nz):
        z_arrival(k).wait_recv()
    for p in range(2):
        rows8 = [ours[p * (nz // 2) + t].astype(jnp.float32) for t in range(nz // 2)]
        packed = [jnp.concatenate([r[:8], r[8:]], axis=1) for r in rows8]
        start = pl.multiple_of(minor[p] * slab, 16)
        cand[p, c, major[p], pl.ds(start, slab), :] = jnp.concatenate(packed, axis=0).astype(
            jnp.bfloat16
        )

    def slab_at(p, a, b, core):
        start = pl.multiple_of(b * slab, 16)
        return cand.at[p, core, a, pl.ds(start, slab), :]

    def spot(p, a, b):
        return (b, a) if p == 0 else (a, b)

    def copy(p, a, b, core, ssem, rsem, target):
        ref = slab_at(p, a, b, core)
        return remote(ref, ref, ssem, rsem, target)

    def major_copy(p, k):
        a, b = major[p], minor[p]
        tx, ty = spot(p, (a + k) % 4, b)
        return copy(p, a, b, c, bs.at[p, k - 1], slab_r.at[p, a, b], device(tx, ty, c, z))

    def minor_copy(p, a, k):
        b = minor[p]
        tx, ty = spot(p, major[p], (b + k) % 4)
        return copy(p, a, b, c, cs.at[p, a, k - 1], slab_r.at[p, a, b], device(tx, ty, c, z))

    def core_copy(p, a):
        ref = cand.at[p, c, a]
        return remote(ref, ref, ks.at[p, a], sib_r.at[p, a], device(x, y, 1 - c, z))

    def slab_arrival(p, a, b):
        return copy(p, a, b, c, ks.at[p, a], slab_r.at[p, a, b], device(x, y, 1 - c, z))

    def core_arrival(p, a):
        ref = cand.at[p, 1 - c, a]
        return remote(ref, ref, ks.at[p, a], sib_r.at[p, a], device(x, y, 1 - c, z))

    for k in (2, 1, 3):
        for p in range(2):
            major_copy(p, k).start()
    for p in range(2):
        for k in (2, 1, 3):
            minor_copy(p, major[p], k).start()
    for k in (1, 3, 2):
        for p in range(2):
            a = (major[p] + k) % 4
            slab_arrival(p, a, minor[p]).wait_recv()
            for j in (2, 1, 3):
                minor_copy(p, a, j).start()

    def pass_on(p, k):
        a = (major[p] + k) % 4
        for j in (1, 3, 2):
            b = (minor[p] + j) % 4
            slab_arrival(p, a, b).wait_recv()
        core_copy(p, a).start()

    def absorb(k):
        at = [(major[p] + k) % 4 for p in range(2)]
        for p in range(2):
            core_arrival(p, at[p]).wait_recv()
        blocks = [jnp.concatenate([cand[p, h, at[p]] for p in range(2)], axis=0) for h in range(2)]
        wide = [block.astype(jnp.float32) for block in blocks]
        norm = jnp.sum(wide[0] * wide[0] + wide[1] * wide[1], axis=1, keepdims=True) * 0.25
        for j in range(rows // TILE):
            lanes = slice(TILE * j, TILE * (j + 1))
            mine = emb[TILE // 16 * j : TILE // 16 * (j + 1)].reshape(TILE, -1)
            product = sum(
                lax.dot_general(
                    blocks[h], mine[:, half * h : half * (h + 1)], NT,
                    preferred_element_type=jnp.float32)
                for h in range(2)
            )
            reach = jnp.min((product + norm).reshape(2, -1, 8, TILE), axis=1)
            least[:, :, lanes] = jnp.minimum(least[:, :, lanes], reach)

    def pass_both(k):
        for p in range(2):
            pass_on(p, k)

    pass_both(0)
    absorb(0)
    pass_both(1)
    pass_both(3)
    absorb(1)
    pass_both(2)
    absorb(3)
    absorb(2)
    load_near.wait()

    norms = out_ref[...]
    near = near_ref[...]
    sums = []
    for p in range(2):
        reach = jnp.min(least[p], axis=0, keepdims=True)
        near = jnp.minimum(near, jnp.maximum(norms + reach, 0.0))
        sums.append(jnp.sum(near, axis=1, keepdims=True))
    lane = lax.broadcasted_iota(jnp.int32, (1, 128), 1)
    share = jnp.where(lane == 0, sums[0], jnp.where(lane == 1, sums[1], 0.0))

    sums_at[position] = share
    everyone = far_first((NX, NY, nz, 2))
    xs, ys = [(x + i) % NX for i in range(NX)], [(y + i) % NY for i in range(NY)]
    zs_, cores = [(z + i) % nz for i in range(nz)], [c, 1 - c]
    for dx, dy, dz, dc in everyone:
        target = device(xs[dx], ys[dy], cores[dc], zs_[dz])
        remote(sums_at.at[position], sums_at.at[position], sum_sem.at[0], sum_sem.at[1], target).start()
    out_ref[...] = near
    store = pltpu.make_async_copy(out_ref, result.at[:, pl.ds(0, rows)], in_sem.at[0])
    store.start()

    for i in range(len(column)):
        slots_copy(i).wait_send()
    for i in range(len(plane)):
        part_copy(i).wait_send()
    for k in range(1, nz):
        z_copy(k).wait_send()
    for p in range(2):
        for k in (1, 2, 3):
            major_copy(p, k).wait_send()
        for a in range(4):
            for k in (1, 2, 3):
                minor_copy(p, a, k).wait_send()
            core_copy(p, a).wait_send()
    others = sums_at.at[pl.ds(0, len(everyone))]
    both = remote(others, others, sum_sem.at[0], sum_sem.at[1], device(x, y, 1 - c, z))
    both.wait_recv()
    total[...] = jnp.sum(sums_at[...], axis=0) / total_rows
    last = pltpu.make_async_copy(total, result.at[:, pl.ds(rows, 128)], in_sem.at[1])
    last.start()
    both.wait_send()
    store.wait()
    last.wait()


def finish(result, near_out, cost_out):
    rows = near_out.shape[1]
    near_out[...] = result[:, :rows]
    cost_out[0] = result[0, rows]
    cost_out[1] = result[0, rows + 1]


def local(embeddings, nearest, chosen):
    rows, width = embeddings.shape
    nz = lax.axis_size("dev")
    total_rows = rows * nz * lax.axis_size("group")
    dma = pltpu.SemaphoreType.DMA

    result = pl.pallas_call(
        functools.partial(kernel, total_rows=total_rows),
        out_shape=jax.ShapeDtypeStruct((1, rows + 128), jnp.float32),
        in_specs=[
            pl.BlockSpec(memory_space=pl.ANY),
            pl.BlockSpec(memory_space=pl.ANY),
            pl.BlockSpec(memory_space=pl.ANY),
        ],
        out_specs=pl.BlockSpec(memory_space=pl.ANY),
        scratch_shapes=[
            pltpu.VMEM((1, rows), jnp.float32),
            pltpu.VMEM(chosen.shape, jnp.int32),
            pltpu.VMEM((1, rows), jnp.float32),
            pltpu.VMEM((rows // 16, 16, width), jnp.bfloat16),
            pltpu.VMEM((2, 16, 3 * width // 8), jnp.bfloat16),
            pltpu.VMEM((2 * nz, 16, 3 * width // 8), jnp.bfloat16),
            pltpu.VMEM((NX * NY, 16, width // 4), jnp.bfloat16),
            pltpu.VMEM((NX * NY, 16, width // 4), jnp.bfloat16),
            pltpu.VMEM((nz, 16, width // 4), jnp.bfloat16),
            pltpu.VMEM((2, 2, 4, 16 * nz, width // 2), jnp.bfloat16),
            pltpu.VMEM((2, 8, rows), jnp.float32),
            pltpu.VMEM((2 * NX * NY * nz, 1, 128), jnp.float32),
            pltpu.VMEM((1, 128), jnp.float32),
            dma((3,)),
            dma((2 * nz - 1,)),
            dma((2 * nz,)),
            dma((NX * NY - 1,)),
            dma((NX * NY,)),
            dma((nz - 1,)),
            dma((nz,)),
            dma((2, 3)),
            dma((2, 4, 3)),
            dma((2, 4)),
            dma((2, 4, 4)),
            dma((2, 4)),
            dma((2,)),
        ],
        compiler_params=pltpu.CompilerParams(
            collective_id=0, has_side_effects=True, vmem_limit_bytes=60 * 2**20
        ),
        cost_estimate=pl.CostEstimate(
            flops=4 * rows * width * chosen.shape[1], bytes_accessed=rows * width * 2, transcendentals=0
        ),
    )(chosen, nearest.reshape(1, rows), embeddings.reshape(rows // 16, 16, width))
    near, cost = pl.pallas_call(
        finish,
        out_shape=(
            jax.ShapeDtypeStruct((1, rows), jnp.float32),
            jax.ShapeDtypeStruct((2,), jnp.float32),
        ),
        in_specs=[
            pl.BlockSpec(memory_space=pltpu.VMEM),
        ],
        out_specs=(
            pl.BlockSpec(memory_space=pltpu.VMEM),
            pl.BlockSpec(memory_space=pltpu.SMEM),
        ),
        compiler_params=pltpu.CompilerParams(vmem_limit_bytes=60 * 2**20),
    )(result)
    return near.reshape(rows), cost


def solution(mesh):
    return jax.shard_map(
        local,
        mesh=mesh,
        in_specs=(P(("group", "dev"), None), P(("group", "dev")), P()),
        out_specs=(P(("group", "dev")), P()),
        check_vma=False,
    )
```

```python
import functools
import itertools

import jax
import jax.numpy as jnp
from jax import lax
from jax.experimental import pallas as pl
from jax.experimental.pallas import tpu as pltpu
from jax.sharding import PartitionSpec as P

MESH = pl.DeviceIdType.MESH
NT = (((1,), (1,)), ((), ()))
NX, NY = 4, 4
MOST = 6
NONE = 2**30
TILE = 512


def far_first(sizes):
    steps = [s for s in itertools.product(*map(range, sizes)) if any(s)]
    return sorted(steps, key=lambda s: -sum(min(a, n - a) for a, n in zip(s, sizes)))


PLANE = far_first((NX, NY))


def place():
    group = lax.axis_index("group")
    return group // (2 * NY), (group // 2) % NY, group % 2, lax.axis_index("dev")


def device(x, y, c, z):
    return ((x * NY + y) * 2 + c, z)


def find_picks(chosen, position, rows):
    cands = chosen.shape[1]
    order = lax.broadcasted_iota(jnp.int32, chosen.shape, 1)
    within = chosen - position * rows
    owned = (within >= 0) & (within < rows)
    key = jnp.where(owned, within * cands + order, NONE)
    found = []
    for _ in range(MOST):
        least = jnp.min(key, axis=1, keepdims=True)
        key = jnp.where(key == least, NONE, key)
        index = jnp.minimum(least, rows * cands - 1) // cands
        tile = index // 16
        found.append((tile, index - tile * 16))
    return found


def picked_rows(found, emb_ref):
    line = lax.broadcasted_iota(jnp.int32, (16, emb_ref.shape[2]), 0)
    picked = []
    for turn in range(2):
        for tile, inside in found:
            block = emb_ref[tile[turn, 0]].astype(jnp.float32)
            here = line == inside[turn : turn + 1, :]
            picked.append(jnp.sum(jnp.where(here, block, 0.0), axis=0, keepdims=True) * -2.0)
    return jnp.concatenate(picked, axis=0)


def slot_sources(chosen_ref, x, y, z, rows, nz):
    cands = chosen_ref.shape[1]
    per = 2 * cands // nz
    turn = z // (nz // 2)
    start = (z % (nz // 2)) * per
    every = chosen_ref[0:1, :] * (1 - turn) + chosen_ref[1:2, :] * turn
    order = lax.broadcasted_iota(jnp.int32, (per, cands), 1)
    place_in = lax.broadcasted_iota(jnp.int32, (per, cands), 0) + start
    mine = jnp.sum(jnp.where(order == place_in, every, 0), axis=1, keepdims=True)
    owner = mine // rows
    earlier = (every < mine) | ((every == mine) & (order < place_in))
    rank = jnp.sum(jnp.where((every // rows == owner) & earlier, 1, 0), axis=1, keepdims=True)
    slot = turn * MOST + rank
    group = owner // nz
    source = ((owner - group * nz) * 2 + group % 2) * 16
    here = group // 2 == x * NY + y
    lane = lax.broadcasted_iota(jnp.int32, (per, 32 * nz), 1)
    main = (here & (lane == source + slot)).astype(jnp.bfloat16)
    low = here & (lane == source + 12 + slot % 4)
    tails = [(low & (slot // 4 == i)).astype(jnp.bfloat16) for i in range(3)]
    return main, tails


def kernel(
    chosen_hbm, near_hbm, emb_hbm, near_hbm_out, sums_hbm,
    out_ref, chosen_ref, near_ref, emb, sent, col, parts, shares, ours, cand, least, share_ref,
    in_sem, zs, zr, ps, pr, os, orr, bs, cs, ks, slab_r, sib_r, sum_sem,
):
    x, y, c, z = place()
    nz = lax.axis_size("dev")
    position = lax.axis_index("group") * nz + z
    rows = emb.shape[0] * 16
    slab = 4 * nz
    half = emb.shape[2] // 2
    cut = 3 * half // 4
    at_z, at_xy = z * 2 + c, x * NY + y
    major, minor = (y, x), (x, y)

    load = pltpu.make_async_copy(emb_hbm, emb, in_sem.at[0])
    load_chosen = pltpu.make_async_copy(chosen_hbm, chosen_ref, in_sem.at[1])
    load_near = pltpu.make_async_copy(near_hbm, near_ref, in_sem.at[2])
    load_chosen.start()
    load.start()
    load_near.start()

    column = [((z + dz) % nz, (c + dc) % 2) for dz, dc in far_first((nz, 2))]
    plane = [((x + dx) % NX, (y + dy) % NY) for dx, dy in PLANE]
    barrier = pltpu.get_barrier_semaphore()
    for tz, tc in column:
        pl.semaphore_signal(barrier, inc=1, device_id=device(x, y, tc, tz), device_id_type=MESH)
    for tx, ty in plane:
        pl.semaphore_signal(barrier, inc=1, device_id=device(tx, ty, c, z), device_id_type=MESH)

    least[...] = jnp.full(least.shape, jnp.inf, jnp.float32)
    load_chosen.wait()
    picks = find_picks(chosen_ref[...], position, rows)
    load.wait()
    found = picked_rows(picks, emb)
    for h in range(2):
        wide = found[:, half * h : half * (h + 1)]
        tail = jnp.concatenate([wide[4 * i : 4 * i + 4, cut:] for i in range(3)], axis=1)
        sent[h] = jnp.concatenate([wide[:, :cut], tail], axis=0).astype(jnp.bfloat16)
    col[at_z] = sent[c]
    pl.semaphore_wait(barrier, len(column) + len(plane))

    def remote(src, dst, ssem, rsem, target):
        return pltpu.make_async_remote_copy(
            src_ref=src, dst_ref=dst, send_sem=ssem, recv_sem=rsem,
            device_id=target, device_id_type=MESH)

    def slots_copy(i):
        tz, tc = column[i]
        return remote(sent.at[tc], col.at[at_z], zs.at[i], zr.at[at_z], device(x, y, tc, tz))

    def slots_arrival(i):
        tz, tc = column[i]
        t = tz * 2 + tc
        return remote(sent.at[tc], col.at[t], zs.at[i], zr.at[t], device(x, y, tc, tz))

    for i in range(len(column)):
        slots_copy(i).start()

    for j in range(rows // 128):
        part = emb[8 * j : 8 * (j + 1)].reshape(128, -1).astype(jnp.float32)
        part = part * part
        part = sum(part[:, 128 * i : 128 * (i + 1)] for i in range(part.shape[1] // 128))
        out_ref[:, 128 * j : 128 * (j + 1)] = jnp.sum(part.T, axis=0, keepdims=True)

    main, tails = slot_sources(chosen_ref, x, y, z, rows, nz)
    for i in range(len(column)):
        slots_arrival(i).wait_recv()

    gathered = col[...].reshape(-1, cut)
    left = jnp.dot(main, gathered, preferred_element_type=jnp.float32)
    right = sum(
        jnp.dot(tail, gathered[:, 128 * i : 128 * (i + 1)], preferred_element_type=jnp.float32)
        for i, tail in enumerate(tails)
    )
    dense = jnp.concatenate([left, right], axis=1)
    for t in range(NX * NY):
        rows8 = dense[8 * t : 8 * t + 8]
        both = jnp.concatenate([rows8[:, : half // 2], rows8[:, half // 2 :]], axis=0)
        parts[t] = both.astype(jnp.bfloat16)
    shares[at_xy] = parts[at_xy]

    def part_copy(i):
        tx, ty = plane[i]
        t = tx * NY + ty
        return remote(parts.at[t], shares.at[at_xy], ps.at[i], pr.at[at_xy], device(tx, ty, c, z))

    def part_arrival(i):
        tx, ty = plane[i]
        t = tx * NY + ty
        return remote(parts.at[t], shares.at[t], ps.at[i], pr.at[t], device(tx, ty, c, z))

    for i in range(len(plane)):
        part_copy(i).start()
    for i in range(len(plane)):
        part_arrival(i).wait_recv()
    ours[z] = jnp.sum(shares[...].astype(jnp.float32), axis=0).astype(jnp.bfloat16)

    def z_copy(k):
        return remote(ours.at[z], ours.at[z], os.at[k - 1], orr.at[z], device(x, y, c, (z + k) % nz))

    def z_arrival(k):
        t = (z + k) % nz
        return remote(ours.at[t], ours.at[t], os.at[k - 1], orr.at[t], device(x, y, c, t))

    for k in (4, 3, 5, 2, 6, 1, 7):
        z_copy(k).start()
    for k in range(1, nz):
        z_arrival(k).wait_recv()
    for p in range(2):
        rows8 = [ours[p * (nz // 2) + t].astype(jnp.float32) for t in range(nz // 2)]
        packed = [jnp.concatenate([r[:8], r[8:]], axis=1) for r in rows8]
        start = pl.multiple_of(minor[p] * slab, 16)
        cand[p, c, major[p], pl.ds(start, slab), :] = jnp.concatenate(packed, axis=0).astype(
            jnp.bfloat16
        )

    def slab_at(p, a, b, core):
        start = pl.multiple_of(b * slab, 16)
        return cand.at[p, core, a, pl.ds(start, slab), :]

    def spot(p, a, b):
        return (b, a) if p == 0 else (a, b)

    def copy(p, a, b, core, ssem, rsem, target):
        ref = slab_at(p, a, b, core)
        return remote(ref, ref, ssem, rsem, target)

    def major_copy(p, k):
        a, b = major[p], minor[p]
        tx, ty = spot(p, (a + k) % 4, b)
        return copy(p, a, b, c, bs.at[p, k - 1], slab_r.at[p, a, b], device(tx, ty, c, z))

    def minor_copy(p, a, k):
        b = minor[p]
        tx, ty = spot(p, major[p], (b + k) % 4)
        return copy(p, a, b, c, cs.at[p, a, k - 1], slab_r.at[p, a, b], device(tx, ty, c, z))

    def core_copy(p, a):
        ref = cand.at[p, c, a]
        return remote(ref, ref, ks.at[p, a], sib_r.at[p, a], device(x, y, 1 - c, z))

    def slab_arrival(p, a, b):
        return copy(p, a, b, c, ks.at[p, a], slab_r.at[p, a, b], device(x, y, 1 - c, z))

    def core_arrival(p, a):
        ref = cand.at[p, 1 - c, a]
        return remote(ref, ref, ks.at[p, a], sib_r.at[p, a], device(x, y, 1 - c, z))

    for k in (2, 1, 3):
        for p in range(2):
            major_copy(p, k).start()
    for p in range(2):
        for k in (2, 1, 3):
            minor_copy(p, major[p], k).start()
    for k in (1, 3, 2):
        for p in range(2):
            a = (major[p] + k) % 4
            slab_arrival(p, a, minor[p]).wait_recv()
            for j in (2, 1, 3):
                minor_copy(p, a, j).start()

    def pass_on(p, k):
        a = (major[p] + k) % 4
        for j in (1, 3, 2):
            b = (minor[p] + j) % 4
            slab_arrival(p, a, b).wait_recv()
        core_copy(p, a).start()

    def absorb(k):
        at = [(major[p] + k) % 4 for p in range(2)]
        for p in range(2):
            core_arrival(p, at[p]).wait_recv()
        blocks = [jnp.concatenate([cand[p, h, at[p]] for p in range(2)], axis=0) for h in range(2)]
        wide = [block.astype(jnp.float32) for block in blocks]
        norm = jnp.sum(wide[0] * wide[0] + wide[1] * wide[1], axis=1, keepdims=True) * 0.25
        for j in range(rows // TILE):
            lanes = slice(TILE * j, TILE * (j + 1))
            mine = emb[TILE // 16 * j : TILE // 16 * (j + 1)].reshape(TILE, -1)
            product = sum(
                lax.dot_general(
                    blocks[h], mine[:, half * h : half * (h + 1)], NT,
                    preferred_element_type=jnp.float32)
                for h in range(2)
            )
            reach = jnp.min((product + norm).reshape(2, -1, 8, TILE), axis=1)
            least[:, :, lanes] = jnp.minimum(least[:, :, lanes], reach)

    def pass_both(k):
        for p in range(2):
            pass_on(p, k)

    pass_both(0)
    absorb(0)
    pass_both(1)
    pass_both(3)
    absorb(1)
    pass_both(2)
    absorb(3)
    absorb(2)
    load_near.wait()

    norms = out_ref[...]
    near = near_ref[...]
    sums = []
    for p in range(2):
        reach = jnp.min(least[p], axis=0, keepdims=True)
        near = jnp.minimum(near, jnp.maximum(norms + reach, 0.0))
        sums.append(jnp.sum(near, axis=1, keepdims=True))
    lane = lax.broadcasted_iota(jnp.int32, (1, 128), 1)
    share = jnp.where(lane == 0, sums[0], jnp.where(lane == 1, sums[1], 0.0))

    share_ref[...] = share
    mine_at = sums_hbm.at[pl.ds(position, 1)]
    keep = pltpu.make_async_copy(share_ref, mine_at, in_sem.at[1])
    everyone = far_first((NX, NY, nz, 2))
    xs, ys = [(x + i) % NX for i in range(NX)], [(y + i) % NY for i in range(NY)]
    zs_, cores = [(z + i) % nz for i in range(nz)], [c, 1 - c]
    for dx, dy, dz, dc in everyone:
        target = device(xs[dx], ys[dy], cores[dc], zs_[dz])
        remote(share_ref, mine_at, sum_sem.at[0], sum_sem.at[1], target).start()
    keep.start()
    out_ref[...] = near
    store = pltpu.make_async_copy(out_ref, near_hbm_out, in_sem.at[0])
    store.start()

    for i in range(len(column)):
        slots_copy(i).wait_send()
    for i in range(len(plane)):
        part_copy(i).wait_send()
    for k in range(1, nz):
        z_copy(k).wait_send()
    for p in range(2):
        for k in (1, 2, 3):
            major_copy(p, k).wait_send()
        for a in range(4):
            for k in (1, 2, 3):
                minor_copy(p, a, k).wait_send()
            core_copy(p, a).wait_send()
    others = sums_hbm.at[pl.ds(0, len(everyone))]
    both = remote(others, others, sum_sem.at[0], sum_sem.at[1], device(x, y, 1 - c, z))
    keep.wait()
    store.wait()
    both.wait_send()
    both.wait_recv()


def finish(near_ref, sums_ref, near_out, cost_out, *, total_rows):
    near_out[...] = near_ref[...]
    total = jnp.sum(sums_ref[...], axis=0, keepdims=True) / total_rows
    cost_out[0] = total[0, 0]
    cost_out[1] = total[0, 1]


def local(embeddings, nearest, chosen):
    rows, width = embeddings.shape
    nz = lax.axis_size("dev")
    total_rows = rows * nz * lax.axis_size("group")
    dma = pltpu.SemaphoreType.DMA

    near, sums = pl.pallas_call(
        kernel,
        out_shape=(
            jax.ShapeDtypeStruct((1, rows), jnp.float32),
            jax.ShapeDtypeStruct((total_rows // rows, 128), jnp.float32),
        ),
        in_specs=[
            pl.BlockSpec(memory_space=pl.ANY),
            pl.BlockSpec(memory_space=pl.ANY),
            pl.BlockSpec(memory_space=pl.ANY),
        ],
        out_specs=(
            pl.BlockSpec(memory_space=pl.ANY),
            pl.BlockSpec(memory_space=pl.ANY),
        ),
        scratch_shapes=[
            pltpu.VMEM((1, rows), jnp.float32),
            pltpu.VMEM(chosen.shape, jnp.int32),
            pltpu.VMEM((1, rows), jnp.float32),
            pltpu.VMEM((rows // 16, 16, width), jnp.bfloat16),
            pltpu.VMEM((2, 16, 3 * width // 8), jnp.bfloat16),
            pltpu.VMEM((2 * nz, 16, 3 * width // 8), jnp.bfloat16),
            pltpu.VMEM((NX * NY, 16, width // 4), jnp.bfloat16),
            pltpu.VMEM((NX * NY, 16, width // 4), jnp.bfloat16),
            pltpu.VMEM((nz, 16, width // 4), jnp.bfloat16),
            pltpu.VMEM((2, 2, 4, 16 * nz, width // 2), jnp.bfloat16),
            pltpu.VMEM((2, 8, rows), jnp.float32),
            pltpu.VMEM((1, 128), jnp.float32),
            dma((3,)),
            dma((2 * nz - 1,)),
            dma((2 * nz,)),
            dma((NX * NY - 1,)),
            dma((NX * NY,)),
            dma((nz - 1,)),
            dma((nz,)),
            dma((2, 3)),
            dma((2, 4, 3)),
            dma((2, 4)),
            dma((2, 4, 4)),
            dma((2, 4)),
            dma((2,)),
        ],
        compiler_params=pltpu.CompilerParams(
            collective_id=0, has_side_effects=True, vmem_limit_bytes=60 * 2**20
        ),
        cost_estimate=pl.CostEstimate(
            flops=4 * rows * width * chosen.shape[1], bytes_accessed=rows * width * 2, transcendentals=0
        ),
    )(chosen, nearest.reshape(1, rows), embeddings.reshape(rows // 16, 16, width))
    near, cost = pl.pallas_call(
        functools.partial(finish, total_rows=total_rows),
        out_shape=(
            jax.ShapeDtypeStruct((1, rows), jnp.float32),
            jax.ShapeDtypeStruct((2,), jnp.float32),
        ),
        in_specs=[
            pl.BlockSpec(memory_space=pltpu.VMEM),
            pl.BlockSpec(memory_space=pltpu.VMEM),
        ],
        out_specs=(
            pl.BlockSpec(memory_space=pltpu.VMEM),
            pl.BlockSpec(memory_space=pltpu.SMEM),
        ),
        compiler_params=pltpu.CompilerParams(vmem_limit_bytes=60 * 2**20),
    )(near, sums)
    return near.reshape(rows), cost


def solution(mesh):
    return jax.shard_map(
        local,
        mesh=mesh,
        in_specs=(P(("group", "dev"), None), P(("group", "dev")), P()),
        out_specs=(P(("group", "dev")), P()),
        check_vma=False,
    )
```

```python
import functools
import itertools

import jax
import jax.numpy as jnp
from jax import lax
from jax.experimental import pallas as pl
from jax.experimental.pallas import tpu as pltpu
from jax.sharding import PartitionSpec as P

MESH = pl.DeviceIdType.MESH
NT = (((1,), (1,)), ((), ()))
NX, NY = 4, 4
MOST = 6
NONE = 2**30
TILE = 512


def far_first(sizes):
    steps = [s for s in itertools.product(*map(range, sizes)) if any(s)]
    return sorted(steps, key=lambda s: -sum(min(a, n - a) for a, n in zip(s, sizes)))


PLANE = far_first((NX, NY))


def place():
    group = lax.axis_index("group")
    return group // (2 * NY), (group // 2) % NY, group % 2, lax.axis_index("dev")


def device(x, y, c, z):
    return ((x * NY + y) * 2 + c, z)


def find_picks(chosen, position, rows):
    cands = chosen.shape[1]
    order = lax.broadcasted_iota(jnp.int32, chosen.shape, 1)
    within = chosen - position * rows
    owned = (within >= 0) & (within < rows)
    key = jnp.where(owned, within * cands + order, NONE)
    found = []
    for _ in range(MOST):
        least = jnp.min(key, axis=1, keepdims=True)
        key = jnp.where(key == least, NONE, key)
        index = jnp.minimum(least, rows * cands - 1) // cands
        tile = index // 16
        found.append((tile, index - tile * 16))
    return found


def picked_rows(found, emb_ref):
    line = lax.broadcasted_iota(jnp.int32, (16, emb_ref.shape[2]), 0)
    picked = []
    for turn in range(2):
        for tile, inside in found:
            block = emb_ref[tile[turn, 0]].astype(jnp.float32)
            here = line == inside[turn : turn + 1, :]
            picked.append(jnp.sum(jnp.where(here, block, 0.0), axis=0, keepdims=True) * -2.0)
    return jnp.concatenate(picked, axis=0)


def slot_sources(chosen_ref, x, y, z, rows, nz):
    cands = chosen_ref.shape[1]
    per = 2 * cands // nz
    turn = z // (nz // 2)
    start = (z % (nz // 2)) * per
    every = chosen_ref[0:1, :] * (1 - turn) + chosen_ref[1:2, :] * turn
    order = lax.broadcasted_iota(jnp.int32, (per, cands), 1)
    place_in = lax.broadcasted_iota(jnp.int32, (per, cands), 0) + start
    mine = jnp.sum(jnp.where(order == place_in, every, 0), axis=1, keepdims=True)
    owner = mine // rows
    earlier = (every < mine) | ((every == mine) & (order < place_in))
    rank = jnp.sum(jnp.where((every // rows == owner) & earlier, 1, 0), axis=1, keepdims=True)
    slot = turn * MOST + rank
    group = owner // nz
    source = ((owner - group * nz) * 2 + group % 2) * 16
    here = group // 2 == x * NY + y
    lane = lax.broadcasted_iota(jnp.int32, (per, 32 * nz), 1)
    main = (here & (lane == source + slot)).astype(jnp.bfloat16)
    low = here & (lane == source + 12 + slot % 4)
    tails = [(low & (slot // 4 == i)).astype(jnp.bfloat16) for i in range(3)]
    return main, tails


def kernel(
    chosen_hbm, near_hbm, emb_hbm, near_hbm_out, sums_hbm,
    out_ref, chosen_ref, near_ref, emb, sent, col, parts, shares, ours, cand, least, share_ref,
    in_sem, zs, ps, os, bs, cs, ks, major_r, minor_r, sib_r, sum_sem,
):
    x, y, c, z = place()
    nz = lax.axis_size("dev")
    position = lax.axis_index("group") * nz + z
    rows = emb.shape[0] * 16
    slab = 4 * nz
    half = emb.shape[2] // 2
    cut = 3 * half // 4
    at_z, at_xy = z * 2 + c, x * NY + y
    major, minor = (y, x), (x, y)

    load = pltpu.make_async_copy(emb_hbm, emb, in_sem.at[0])
    load_chosen = pltpu.make_async_copy(chosen_hbm, chosen_ref, in_sem.at[1])
    load_near = pltpu.make_async_copy(near_hbm, near_ref, in_sem.at[2])
    load_chosen.start()
    load.start()
    load_near.start()

    column = [((z + dz) % nz, (c + dc) % 2) for dz, dc in far_first((nz, 2))]
    plane = [((x + dx) % NX, (y + dy) % NY) for dx, dy in PLANE]
    barrier = pltpu.get_barrier_semaphore()
    for tz, tc in column:
        pl.semaphore_signal(barrier, inc=1, device_id=device(x, y, tc, tz), device_id_type=MESH)
    for tx, ty in plane:
        pl.semaphore_signal(barrier, inc=1, device_id=device(tx, ty, c, z), device_id_type=MESH)

    least[...] = jnp.full(least.shape, jnp.inf, jnp.float32)
    load_chosen.wait()
    picks = find_picks(chosen_ref[...], position, rows)
    load.wait()
    found = picked_rows(picks, emb)
    for h in range(2):
        wide = found[:, half * h : half * (h + 1)]
        tail = jnp.concatenate([wide[4 * i : 4 * i + 4, cut:] for i in range(3)], axis=1)
        sent[h] = jnp.concatenate([wide[:, :cut], tail], axis=0).astype(jnp.bfloat16)
    col[at_z] = sent[c]
    pl.semaphore_wait(barrier, len(column) + len(plane))

    def remote(src, dst, ssem, rsem, target):
        return pltpu.make_async_remote_copy(
            src_ref=src, dst_ref=dst, send_sem=ssem, recv_sem=rsem,
            device_id=target, device_id_type=MESH)

    def drain(ref, sems):
        return remote(ref, ref, sems.at[0], sems.at[1], device(x, y, 1 - c, z))

    for tz, tc in column:
        remote(sent.at[tc], col.at[at_z], zs.at[0], zs.at[1], device(x, y, tc, tz)).start()
    slots = drain(col.at[pl.ds(0, len(column))], zs)

    for j in range(rows // 128):
        part = emb[8 * j : 8 * (j + 1)].reshape(128, -1).astype(jnp.float32)
        part = part * part
        part = sum(part[:, 128 * i : 128 * (i + 1)] for i in range(part.shape[1] // 128))
        out_ref[:, 128 * j : 128 * (j + 1)] = jnp.sum(part.T, axis=0, keepdims=True)

    main, tails = slot_sources(chosen_ref, x, y, z, rows, nz)
    slots.wait_recv()

    gathered = col[...].reshape(-1, cut)
    left = jnp.dot(main, gathered, preferred_element_type=jnp.float32)
    right = sum(
        jnp.dot(tail, gathered[:, 128 * i : 128 * (i + 1)], preferred_element_type=jnp.float32)
        for i, tail in enumerate(tails)
    )
    dense = jnp.concatenate([left, right], axis=1)
    for t in range(NX * NY):
        rows8 = dense[8 * t : 8 * t + 8]
        both = jnp.concatenate([rows8[:, : half // 2], rows8[:, half // 2 :]], axis=0)
        parts[t] = both.astype(jnp.bfloat16)
    shares[at_xy] = parts[at_xy]

    for tx, ty in plane:
        t = tx * NY + ty
        remote(parts.at[t], shares.at[at_xy], ps.at[0], ps.at[1], device(tx, ty, c, z)).start()
    part = drain(shares.at[pl.ds(0, len(plane))], ps)
    part.wait_recv()
    ours[z] = jnp.sum(shares[...].astype(jnp.float32), axis=0).astype(jnp.bfloat16)

    for k in (4, 3, 5, 2, 6, 1, 7):
        remote(ours.at[z], ours.at[z], os.at[0], os.at[1], device(x, y, c, (z + k) % nz)).start()
    along = drain(ours.at[pl.ds(0, nz - 1)], os)
    along.wait_recv()
    for p in range(2):
        rows8 = [ours[p * (nz // 2) + t].astype(jnp.float32) for t in range(nz // 2)]
        packed = [jnp.concatenate([r[:8], r[8:]], axis=1) for r in rows8]
        start = pl.multiple_of(minor[p] * slab, 16)
        cand[p, c, major[p], pl.ds(start, slab), :] = jnp.concatenate(packed, axis=0).astype(
            jnp.bfloat16
        )

    def slab_at(p, a, b, core):
        start = pl.multiple_of(b * slab, 16)
        return cand.at[p, core, a, pl.ds(start, slab), :]

    def spot(p, a, b):
        return (b, a) if p == 0 else (a, b)

    def copy(p, a, b, core, ssem, rsem, target):
        ref = slab_at(p, a, b, core)
        return remote(ref, ref, ssem, rsem, target)

    def major_copy(p, k):
        a, b = major[p], minor[p]
        tx, ty = spot(p, (a + k) % 4, b)
        return copy(p, a, b, c, bs.at[p], major_r.at[p, a], device(tx, ty, c, z))

    def minor_copy(p, a, k):
        b = minor[p]
        tx, ty = spot(p, major[p], (b + k) % 4)
        return copy(p, a, b, c, cs.at[p], minor_r.at[p, a], device(tx, ty, c, z))

    def core_copy(p, a):
        ref = cand.at[p, c, a]
        return remote(ref, ref, ks.at[p], sib_r.at[p, a], device(x, y, 1 - c, z))

    def major_arrival(p, a):
        return copy(p, a, minor[p], c, bs.at[p], major_r.at[p, a], device(x, y, 1 - c, z))

    def minor_arrivals(p, a):
        ref = cand.at[p, c, a, pl.ds(0, 3 * slab)]
        return remote(ref, ref, cs.at[p], minor_r.at[p, a], device(x, y, 1 - c, z))

    def core_arrival(p, a):
        ref = cand.at[p, 1 - c, a]
        return remote(ref, ref, ks.at[p], sib_r.at[p, a], device(x, y, 1 - c, z))

    for k in (2, 1, 3):
        for p in range(2):
            major_copy(p, k).start()
    for p in range(2):
        for k in (2, 1, 3):
            minor_copy(p, major[p], k).start()
    for k in (1, 3, 2):
        for p in range(2):
            a = (major[p] + k) % 4
            major_arrival(p, a).wait_recv()
            for j in (2, 1, 3):
                minor_copy(p, a, j).start()

    def pass_on(p, k):
        a = (major[p] + k) % 4
        minor_arrivals(p, a).wait_recv()
        core_copy(p, a).start()

    def absorb(k):
        at = [(major[p] + k) % 4 for p in range(2)]
        for p in range(2):
            core_arrival(p, at[p]).wait_recv()
        blocks = [jnp.concatenate([cand[p, h, at[p]] for p in range(2)], axis=0) for h in range(2)]
        wide = [block.astype(jnp.float32) for block in blocks]
        norm = jnp.sum(wide[0] * wide[0] + wide[1] * wide[1], axis=1, keepdims=True) * 0.25
        for j in range(rows // TILE):
            lanes = slice(TILE * j, TILE * (j + 1))
            mine = emb[TILE // 16 * j : TILE // 16 * (j + 1)].reshape(TILE, -1)
            product = sum(
                lax.dot_general(
                    blocks[h], mine[:, half * h : half * (h + 1)], NT,
                    preferred_element_type=jnp.float32)
                for h in range(2)
            )
            reach = jnp.min((product + norm).reshape(2, -1, 8, TILE), axis=1)
            least[:, :, lanes] = jnp.minimum(least[:, :, lanes], reach)

    def pass_both(k):
        for p in range(2):
            pass_on(p, k)

    pass_both(0)
    absorb(0)
    pass_both(1)
    pass_both(3)
    absorb(1)
    pass_both(2)
    absorb(3)
    absorb(2)
    load_near.wait()

    norms = out_ref[...]
    near = near_ref[...]
    sums = []
    for p in range(2):
        reach = jnp.min(least[p], axis=0, keepdims=True)
        near = jnp.minimum(near, jnp.maximum(norms + reach, 0.0))
        sums.append(jnp.sum(near, axis=1, keepdims=True))
    lane = lax.broadcasted_iota(jnp.int32, (1, 128), 1)
    share = jnp.where(lane == 0, sums[0], jnp.where(lane == 1, sums[1], 0.0))

    share_ref[...] = share
    mine_at = sums_hbm.at[pl.ds(position, 1)]
    keep = pltpu.make_async_copy(share_ref, mine_at, in_sem.at[1])
    everyone = far_first((NX, NY, nz, 2))
    xs, ys = [(x + i) % NX for i in range(NX)], [(y + i) % NY for i in range(NY)]
    zs_, cores = [(z + i) % nz for i in range(nz)], [c, 1 - c]
    for dx, dy, dz, dc in everyone:
        target = device(xs[dx], ys[dy], cores[dc], zs_[dz])
        remote(share_ref, mine_at, sum_sem.at[0], sum_sem.at[1], target).start()
    keep.start()
    out_ref[...] = near
    store = pltpu.make_async_copy(out_ref, near_hbm_out, in_sem.at[0])
    store.start()

    slots.wait_send()
    part.wait_send()
    along.wait_send()
    for p in range(2):
        three = cand.at[p, c, pl.ds(0, 3)]
        first = cand.at[p, c, 0, pl.ds(0, 3 * slab)]
        remote(first, first, bs.at[p], major_r.at[p, 0], device(x, y, 1 - c, z)).wait_send()
        remote(three, three, cs.at[p], minor_r.at[p, 0], device(x, y, 1 - c, z)).wait_send()
        four = cand.at[p, c]
        remote(four, four, ks.at[p], sib_r.at[p, 0], device(x, y, 1 - c, z)).wait_send()
    others = sums_hbm.at[pl.ds(0, len(everyone))]
    both = remote(others, others, sum_sem.at[0], sum_sem.at[1], device(x, y, 1 - c, z))
    keep.wait()
    store.wait()
    both.wait_send()
    both.wait_recv()


def finish(near_ref, sums_ref, near_out, cost_out, *, total_rows):
    near_out[...] = near_ref[...]
    total = jnp.sum(sums_ref[...], axis=0, keepdims=True) / total_rows
    cost_out[0] = total[0, 0]
    cost_out[1] = total[0, 1]


def local(embeddings, nearest, chosen):
    rows, width = embeddings.shape
    nz = lax.axis_size("dev")
    total_rows = rows * nz * lax.axis_size("group")
    dma = pltpu.SemaphoreType.DMA

    near, sums = pl.pallas_call(
        kernel,
        out_shape=(
            jax.ShapeDtypeStruct((1, rows), jnp.float32),
            jax.ShapeDtypeStruct((total_rows // rows, 128), jnp.float32),
        ),
        in_specs=[
            pl.BlockSpec(memory_space=pl.ANY),
            pl.BlockSpec(memory_space=pl.ANY),
            pl.BlockSpec(memory_space=pl.ANY),
        ],
        out_specs=(
            pl.BlockSpec(memory_space=pl.ANY),
            pl.BlockSpec(memory_space=pl.ANY),
        ),
        scratch_shapes=[
            pltpu.VMEM((1, rows), jnp.float32),
            pltpu.VMEM(chosen.shape, jnp.int32),
            pltpu.VMEM((1, rows), jnp.float32),
            pltpu.VMEM((rows // 16, 16, width), jnp.bfloat16),
            pltpu.VMEM((2, 16, 3 * width // 8), jnp.bfloat16),
            pltpu.VMEM((2 * nz, 16, 3 * width // 8), jnp.bfloat16),
            pltpu.VMEM((NX * NY, 16, width // 4), jnp.bfloat16),
            pltpu.VMEM((NX * NY, 16, width // 4), jnp.bfloat16),
            pltpu.VMEM((nz, 16, width // 4), jnp.bfloat16),
            pltpu.VMEM((2, 2, 4, 16 * nz, width // 2), jnp.bfloat16),
            pltpu.VMEM((2, 8, rows), jnp.float32),
            pltpu.VMEM((1, 128), jnp.float32),
            dma((3,)),
            dma((2,)),
            dma((2,)),
            dma((2,)),
            dma((2,)),
            dma((2,)),
            dma((2,)),
            dma((2, 4)),
            dma((2, 4)),
            dma((2, 4)),
            dma((2,)),
        ],
        compiler_params=pltpu.CompilerParams(
            collective_id=0, has_side_effects=True, vmem_limit_bytes=60 * 2**20
        ),
        cost_estimate=pl.CostEstimate(
            flops=4 * rows * width * chosen.shape[1], bytes_accessed=rows * width * 2, transcendentals=0
        ),
    )(chosen, nearest.reshape(1, rows), embeddings.reshape(rows // 16, 16, width))
    near, cost = pl.pallas_call(
        functools.partial(finish, total_rows=total_rows),
        out_shape=(
            jax.ShapeDtypeStruct((1, rows), jnp.float32),
            jax.ShapeDtypeStruct((2,), jnp.float32),
        ),
        in_specs=[
            pl.BlockSpec(memory_space=pltpu.VMEM),
            pl.BlockSpec(memory_space=pltpu.VMEM),
        ],
        out_specs=(
            pl.BlockSpec(memory_space=pltpu.VMEM),
            pl.BlockSpec(memory_space=pltpu.SMEM),
        ),
        compiler_params=pltpu.CompilerParams(vmem_limit_bytes=60 * 2**20),
    )(near, sums)
    return near.reshape(rows), cost


def solution(mesh):
    return jax.shard_map(
        local,
        mesh=mesh,
        in_specs=(P(("group", "dev"), None), P(("group", "dev")), P()),
        out_specs=(P(("group", "dev")), P()),
        check_vma=False,
    )
```

```python
import functools
import itertools

import jax
import jax.numpy as jnp
from jax import lax
from jax.experimental import pallas as pl
from jax.experimental.pallas import tpu as pltpu
from jax.sharding import PartitionSpec as P

MESH = pl.DeviceIdType.MESH
NT = (((1,), (1,)), ((), ()))
NX, NY = 4, 4
MOST = 6
NONE = 2**30
TILE = 512


def far_first(sizes):
    steps = [s for s in itertools.product(*map(range, sizes)) if any(s)]
    return sorted(steps, key=lambda s: -sum(min(a, n - a) for a, n in zip(s, sizes)))


PLANE = far_first((NX, NY))


def place():
    group = lax.axis_index("group")
    return group // (2 * NY), (group // 2) % NY, group % 2, lax.axis_index("dev")


def device(x, y, c, z):
    return ((x * NY + y) * 2 + c, z)


def find_picks(chosen, position, rows):
    cands = chosen.shape[1]
    order = lax.broadcasted_iota(jnp.int32, chosen.shape, 1)
    within = chosen - position * rows
    owned = (within >= 0) & (within < rows)
    key = jnp.where(owned, within * cands + order, NONE)
    found = []
    for _ in range(MOST):
        least = jnp.min(key, axis=1, keepdims=True)
        key = jnp.where(key == least, NONE, key)
        index = jnp.minimum(least, rows * cands - 1) // cands
        tile = index // 16
        found.append((tile, index - tile * 16))
    return found


def picked_rows(found, emb_ref):
    line = lax.broadcasted_iota(jnp.int32, (16, emb_ref.shape[2]), 0)
    picked = []
    for turn in range(2):
        for tile, inside in found:
            block = emb_ref[tile[turn, 0]].astype(jnp.float32)
            here = line == inside[turn : turn + 1, :]
            picked.append(jnp.sum(jnp.where(here, block, 0.0), axis=0, keepdims=True) * -2.0)
    return jnp.concatenate(picked, axis=0)


def slot_sources(chosen_ref, x, y, z, rows, nz):
    cands = chosen_ref.shape[1]
    per = 2 * cands // nz
    turn = z // (nz // 2)
    start = (z % (nz // 2)) * per
    every = chosen_ref[0:1, :] * (1 - turn) + chosen_ref[1:2, :] * turn
    order = lax.broadcasted_iota(jnp.int32, (per, cands), 1)
    place_in = lax.broadcasted_iota(jnp.int32, (per, cands), 0) + start
    mine = jnp.sum(jnp.where(order == place_in, every, 0), axis=1, keepdims=True)
    owner = mine // rows
    earlier = (every < mine) | ((every == mine) & (order < place_in))
    rank = jnp.sum(jnp.where((every // rows == owner) & earlier, 1, 0), axis=1, keepdims=True)
    slot = turn * MOST + rank
    group = owner // nz
    source = ((owner - group * nz) * 2 + group % 2) * 16
    here = group // 2 == x * NY + y
    lane = lax.broadcasted_iota(jnp.int32, (per, 32 * nz), 1)
    main = (here & (lane == source + slot)).astype(jnp.bfloat16)
    low = here & (lane == source + 12 + slot % 4)
    tails = [(low & (slot // 4 == i)).astype(jnp.bfloat16) for i in range(3)]
    return main, tails


def kernel(
    chosen_hbm, near_hbm, emb_hbm, near_hbm_out, sums_hbm,
    out_ref, chosen_ref, near_ref, emb, sent, col, parts, shares, ours, cand, least, share_ref,
    in_sem, zs, ps, os, bs, cs, ks, major_r, minor_r, sib_r, sum_sem,
):
    x, y, c, z = place()
    nz = lax.axis_size("dev")
    position = lax.axis_index("group") * nz + z
    rows = emb.shape[0] * 16
    slab = 4 * nz
    half = emb.shape[2] // 2
    cut = 3 * half // 4
    at_z, at_xy = z * 2 + c, x * NY + y
    major, minor = (y, x), (x, y)

    load = pltpu.make_async_copy(emb_hbm, emb, in_sem.at[0])
    load_chosen = pltpu.make_async_copy(chosen_hbm, chosen_ref, in_sem.at[1])
    load_near = pltpu.make_async_copy(near_hbm, near_ref, in_sem.at[2])
    load_chosen.start()
    load.start()
    load_near.start()

    column = [((z + dz) % nz, (c + dc) % 2) for dz, dc in far_first((nz, 2))]
    plane = [((x + dx) % NX, (y + dy) % NY) for dx, dy in PLANE]
    barrier = pltpu.get_barrier_semaphore()
    for tz, tc in column:
        pl.semaphore_signal(barrier, inc=1, device_id=device(x, y, tc, tz), device_id_type=MESH)
    for tx, ty in plane:
        pl.semaphore_signal(barrier, inc=1, device_id=device(tx, ty, c, z), device_id_type=MESH)

    least[...] = jnp.full(least.shape, jnp.inf, jnp.float32)
    load_chosen.wait()
    picks = find_picks(chosen_ref[...], position, rows)
    load.wait()
    found = picked_rows(picks, emb)
    for h in range(2):
        wide = found[:, half * h : half * (h + 1)]
        tail = jnp.concatenate([wide[4 * i : 4 * i + 4, cut:] for i in range(3)], axis=1)
        sent[h] = jnp.concatenate([wide[:, :cut], tail], axis=0).astype(jnp.bfloat16)
    col[at_z] = sent[c]
    pl.semaphore_wait(barrier, len(column) + len(plane))

    def remote(src, dst, ssem, rsem, target):
        return pltpu.make_async_remote_copy(
            src_ref=src, dst_ref=dst, send_sem=ssem, recv_sem=rsem,
            device_id=target, device_id_type=MESH)

    def drain(ref, sems):
        return remote(ref, ref, sems.at[0], sems.at[1], device(x, y, 1 - c, z))

    for tz, tc in column:
        remote(sent.at[tc], col.at[at_z], zs.at[0], zs.at[1], device(x, y, tc, tz)).start()
    slots = drain(col.at[pl.ds(0, len(column))], zs)

    for j in range(rows // 128):
        part = emb[8 * j : 8 * (j + 1)].reshape(128, -1).astype(jnp.float32)
        part = part * part
        part = sum(part[:, 128 * i : 128 * (i + 1)] for i in range(part.shape[1] // 128))
        out_ref[:, 128 * j : 128 * (j + 1)] = jnp.sum(part.T, axis=0, keepdims=True)

    main, tails = slot_sources(chosen_ref, x, y, z, rows, nz)
    slots.wait_recv()

    gathered = col[...].reshape(-1, cut)
    left = jnp.dot(main, gathered, preferred_element_type=jnp.float32)
    stacked = jnp.concatenate([gathered[:, 128 * i : 128 * (i + 1)] for i in range(3)], axis=0)
    right = jnp.dot(
        jnp.concatenate(tails, axis=1), stacked, preferred_element_type=jnp.float32
    )
    dense = jnp.concatenate([left, right], axis=1)
    for t in range(NX * NY):
        rows8 = dense[8 * t : 8 * t + 8]
        both = jnp.concatenate([rows8[:, : half // 2], rows8[:, half // 2 :]], axis=0)
        parts[t] = both.astype(jnp.bfloat16)
    shares[at_xy] = parts[at_xy]

    for tx, ty in plane:
        t = tx * NY + ty
        remote(parts.at[t], shares.at[at_xy], ps.at[0], ps.at[1], device(tx, ty, c, z)).start()
    part = drain(shares.at[pl.ds(0, len(plane))], ps)
    part.wait_recv()
    ours[z] = jnp.sum(shares[...].astype(jnp.float32), axis=0).astype(jnp.bfloat16)

    for k in (4, 3, 5, 2, 6, 1, 7):
        remote(ours.at[z], ours.at[z], os.at[0], os.at[1], device(x, y, c, (z + k) % nz)).start()
    along = drain(ours.at[pl.ds(0, nz - 1)], os)
    along.wait_recv()
    for p in range(2):
        rows8 = [ours[p * (nz // 2) + t].astype(jnp.float32) for t in range(nz // 2)]
        packed = [jnp.concatenate([r[:8], r[8:]], axis=1) for r in rows8]
        start = pl.multiple_of(minor[p] * slab, 16)
        cand[p, c, major[p], pl.ds(start, slab), :] = jnp.concatenate(packed, axis=0).astype(
            jnp.bfloat16
        )

    def slab_at(p, a, b, core, piece=None):
        start, size = (b * slab, slab) if piece is None else (b * slab + 16 * piece, 16)
        return cand.at[p, core, a, pl.ds(pl.multiple_of(start, 16), size), :]

    def spot(p, a, b):
        return (b, a) if p == 0 else (a, b)

    def copy(p, a, b, core, ssem, rsem, target, piece=None):
        ref = slab_at(p, a, b, core, piece)
        return remote(ref, ref, ssem, rsem, target)

    def major_copy(p, k, h):
        a, b = major[p], minor[p]
        tx, ty = spot(p, (a + k) % 4, b)
        return copy(p, a, b, c, bs.at[p], major_r.at[p, a, h], device(tx, ty, c, z), h)

    def minor_copy(p, a, k, h=None):
        b = minor[p]
        tx, ty = spot(p, major[p], (b + k) % 4)
        return copy(p, a, b, c, cs.at[p], minor_r.at[p, a], device(tx, ty, c, z), h)

    def core_copy(p, a):
        ref = cand.at[p, c, a]
        return remote(ref, ref, ks.at[p], sib_r.at[p, a], device(x, y, 1 - c, z))

    def major_arrival(p, a, h):
        return copy(p, a, minor[p], c, bs.at[p], major_r.at[p, a, h], device(x, y, 1 - c, z), h)

    def minor_arrivals(p, a):
        ref = cand.at[p, c, a, pl.ds(0, 3 * slab)]
        return remote(ref, ref, cs.at[p], minor_r.at[p, a], device(x, y, 1 - c, z))

    def core_arrival(p, a):
        ref = cand.at[p, 1 - c, a]
        return remote(ref, ref, ks.at[p], sib_r.at[p, a], device(x, y, 1 - c, z))

    for h in range(2):
        for k in (2, 1, 3):
            for p in range(2):
                major_copy(p, k, h).start()
    for p in range(2):
        for k in (2, 1, 3):
            minor_copy(p, major[p], k).start()
    for k, h in ((1, 0), (3, 0), (1, 1), (3, 1), (2, 0), (2, 1)):
        for p in range(2):
            a = (major[p] + k) % 4
            major_arrival(p, a, h).wait_recv()
            for j in (2, 1, 3):
                minor_copy(p, a, j, h).start()

    def pass_on(p, k):
        a = (major[p] + k) % 4
        minor_arrivals(p, a).wait_recv()
        core_copy(p, a).start()

    def absorb(k):
        at = [(major[p] + k) % 4 for p in range(2)]
        for p in range(2):
            core_arrival(p, at[p]).wait_recv()
        blocks = [jnp.concatenate([cand[p, h, at[p]] for p in range(2)], axis=0) for h in range(2)]
        wide = [block.astype(jnp.float32) for block in blocks]
        norm = jnp.sum(wide[0] * wide[0] + wide[1] * wide[1], axis=1, keepdims=True) * 0.25
        for j in range(rows // TILE):
            lanes = slice(TILE * j, TILE * (j + 1))
            mine = emb[TILE // 16 * j : TILE // 16 * (j + 1)].reshape(TILE, -1)
            product = sum(
                lax.dot_general(
                    blocks[h], mine[:, half * h : half * (h + 1)], NT,
                    preferred_element_type=jnp.float32)
                for h in range(2)
            )
            reach = jnp.min((product + norm).reshape(2, -1, 8, TILE), axis=1)
            least[:, :, lanes] = jnp.minimum(least[:, :, lanes], reach)

    def pass_both(k):
        for p in range(2):
            pass_on(p, k)

    pass_both(0)
    pass_both(1)
    absorb(0)
    pass_both(3)
    absorb(1)
    pass_both(2)
    absorb(3)
    absorb(2)
    load_near.wait()

    norms = out_ref[...]
    near = near_ref[...]
    sums = []
    for p in range(2):
        reach = jnp.min(least[p], axis=0, keepdims=True)
        near = jnp.minimum(near, jnp.maximum(norms + reach, 0.0))
        sums.append(jnp.sum(near, axis=1, keepdims=True))
    lane = lax.broadcasted_iota(jnp.int32, (1, 128), 1)
    share = jnp.where(lane == 0, sums[0], jnp.where(lane == 1, sums[1], 0.0))

    share_ref[...] = share
    mine_at = sums_hbm.at[pl.ds(position, 1)]
    keep = pltpu.make_async_copy(share_ref, mine_at, in_sem.at[1])
    everyone = far_first((NX, NY, nz, 2))
    xs, ys = [(x + i) % NX for i in range(NX)], [(y + i) % NY for i in range(NY)]
    zs_, cores = [(z + i) % nz for i in range(nz)], [c, 1 - c]
    for dx, dy, dz, dc in everyone:
        target = device(xs[dx], ys[dy], cores[dc], zs_[dz])
        remote(share_ref, mine_at, sum_sem.at[0], sum_sem.at[1], target).start()
    keep.start()
    out_ref[...] = near
    store = pltpu.make_async_copy(out_ref, near_hbm_out, in_sem.at[0])
    store.start()

    slots.wait_send()
    part.wait_send()
    along.wait_send()
    for p in range(2):
        three = cand.at[p, c, pl.ds(0, 3)]
        first = cand.at[p, c, 0, pl.ds(0, 3 * slab)]
        remote(first, first, bs.at[p], major_r.at[p, 0, 0], device(x, y, 1 - c, z)).wait_send()
        remote(three, three, cs.at[p], minor_r.at[p, 0], device(x, y, 1 - c, z)).wait_send()
        four = cand.at[p, c]
        remote(four, four, ks.at[p], sib_r.at[p, 0], device(x, y, 1 - c, z)).wait_send()
    others = sums_hbm.at[pl.ds(0, len(everyone))]
    both = remote(others, others, sum_sem.at[0], sum_sem.at[1], device(x, y, 1 - c, z))
    keep.wait()
    store.wait()
    both.wait_send()
    both.wait_recv()


def finish(near_ref, sums_ref, near_out, cost_out, *, total_rows):
    near_out[...] = near_ref[...]
    total = jnp.sum(sums_ref[...], axis=0, keepdims=True) / total_rows
    cost_out[0] = total[0, 0]
    cost_out[1] = total[0, 1]


def local(embeddings, nearest, chosen):
    rows, width = embeddings.shape
    nz = lax.axis_size("dev")
    total_rows = rows * nz * lax.axis_size("group")
    dma = pltpu.SemaphoreType.DMA

    near, sums = pl.pallas_call(
        kernel,
        out_shape=(
            jax.ShapeDtypeStruct((1, rows), jnp.float32),
            jax.ShapeDtypeStruct((total_rows // rows, 128), jnp.float32),
        ),
        in_specs=[
            pl.BlockSpec(memory_space=pl.ANY),
            pl.BlockSpec(memory_space=pl.ANY),
            pl.BlockSpec(memory_space=pl.ANY),
        ],
        out_specs=(
            pl.BlockSpec(memory_space=pl.ANY),
            pl.BlockSpec(memory_space=pl.ANY),
        ),
        scratch_shapes=[
            pltpu.VMEM((1, rows), jnp.float32),
            pltpu.VMEM(chosen.shape, jnp.int32),
            pltpu.VMEM((1, rows), jnp.float32),
            pltpu.VMEM((rows // 16, 16, width), jnp.bfloat16),
            pltpu.VMEM((2, 16, 3 * width // 8), jnp.bfloat16),
            pltpu.VMEM((2 * nz, 16, 3 * width // 8), jnp.bfloat16),
            pltpu.VMEM((NX * NY, 16, width // 4), jnp.bfloat16),
            pltpu.VMEM((NX * NY, 16, width // 4), jnp.bfloat16),
            pltpu.VMEM((nz, 16, width // 4), jnp.bfloat16),
            pltpu.VMEM((2, 2, 4, 16 * nz, width // 2), jnp.bfloat16),
            pltpu.VMEM((2, 8, rows), jnp.float32),
            pltpu.VMEM((1, 128), jnp.float32),
            dma((3,)),
            dma((2,)),
            dma((2,)),
            dma((2,)),
            dma((2,)),
            dma((2,)),
            dma((2,)),
            dma((2, 4, 2)),
            dma((2, 4)),
            dma((2, 4)),
            dma((2,)),
        ],
        compiler_params=pltpu.CompilerParams(
            collective_id=0, has_side_effects=True, vmem_limit_bytes=60 * 2**20
        ),
        cost_estimate=pl.CostEstimate(
            flops=4 * rows * width * chosen.shape[1], bytes_accessed=rows * width * 2, transcendentals=0
        ),
    )(chosen, nearest.reshape(1, rows), embeddings.reshape(rows // 16, 16, width))
    near, cost = pl.pallas_call(
        functools.partial(finish, total_rows=total_rows),
        out_shape=(
            jax.ShapeDtypeStruct((1, rows), jnp.float32),
            jax.ShapeDtypeStruct((2,), jnp.float32),
        ),
        in_specs=[
            pl.BlockSpec(memory_space=pltpu.VMEM),
            pl.BlockSpec(memory_space=pltpu.VMEM),
        ],
        out_specs=(
            pl.BlockSpec(memory_space=pltpu.VMEM),
            pl.BlockSpec(memory_space=pltpu.SMEM),
        ),
        compiler_params=pltpu.CompilerParams(vmem_limit_bytes=60 * 2**20),
    )(near, sums)
    return near.reshape(rows), cost


def solution(mesh):
    return jax.shard_map(
        local,
        mesh=mesh,
        in_specs=(P(("group", "dev"), None), P(("group", "dev")), P()),
        out_specs=(P(("group", "dev")), P()),
        check_vma=False,
    )
```

```python
import functools
import itertools

import jax
import jax.numpy as jnp
from jax import lax
from jax.experimental import pallas as pl
from jax.experimental.pallas import tpu as pltpu
from jax.sharding import PartitionSpec as P

MESH = pl.DeviceIdType.MESH
NT = (((1,), (1,)), ((), ()))
NX, NY = 4, 4
MOST = 6
NONE = 2**30
TILE = 512


def far_first(sizes):
    steps = [s for s in itertools.product(*map(range, sizes)) if any(s)]
    return sorted(steps, key=lambda s: -sum(min(a, n - a) for a, n in zip(s, sizes)))


PLANE = far_first((NX, NY))


def place():
    group = lax.axis_index("group")
    return group // (2 * NY), (group // 2) % NY, group % 2, lax.axis_index("dev")


def device(x, y, c, z):
    return ((x * NY + y) * 2 + c, z)


def find_picks(chosen, position, rows):
    cands = chosen.shape[1]
    order = lax.broadcasted_iota(jnp.int32, chosen.shape, 1)
    within = chosen - position * rows
    owned = (within >= 0) & (within < rows)
    key = jnp.where(owned, within * cands + order, NONE)
    found = []
    for _ in range(MOST):
        least = jnp.min(key, axis=1, keepdims=True)
        key = jnp.where(key == least, NONE, key)
        index = jnp.minimum(least, rows * cands - 1) // cands
        tile = index // 16
        found.append((tile, index - tile * 16))
    return found


def picked_rows(found, emb_ref):
    line = lax.broadcasted_iota(jnp.int32, (16, emb_ref.shape[2]), 0)
    picked = []
    for turn in range(2):
        for tile, inside in found:
            block = emb_ref[tile[turn, 0]].astype(jnp.float32)
            here = line == inside[turn : turn + 1, :]
            picked.append(jnp.sum(jnp.where(here, block, 0.0), axis=0, keepdims=True) * -2.0)
    return jnp.concatenate(picked, axis=0)


def slot_sources(chosen_ref, x, y, z, rows, nz):
    cands = chosen_ref.shape[1]
    per = 2 * cands // nz
    turn = z // (nz // 2)
    start = (z % (nz // 2)) * per
    every = chosen_ref[0:1, :] * (1 - turn) + chosen_ref[1:2, :] * turn
    order = lax.broadcasted_iota(jnp.int32, (per, cands), 1)
    place_in = lax.broadcasted_iota(jnp.int32, (per, cands), 0) + start
    mine = jnp.sum(jnp.where(order == place_in, every, 0), axis=1, keepdims=True)
    owner = mine // rows
    earlier = (every < mine) | ((every == mine) & (order < place_in))
    rank = jnp.sum(jnp.where((every // rows == owner) & earlier, 1, 0), axis=1, keepdims=True)
    slot = turn * MOST + rank
    group = owner // nz
    source = ((owner - group * nz) * 2 + group % 2) * 16
    here = group // 2 == x * NY + y
    lane = lax.broadcasted_iota(jnp.int32, (per, 32 * nz), 1)
    main = (here & (lane == source + slot)).astype(jnp.bfloat16)
    low = here & (lane == source + 12 + slot % 4)
    tails = [(low & (slot // 4 == i)).astype(jnp.bfloat16) for i in range(3)]
    return main, tails


def kernel(
    chosen_hbm, near_hbm, emb_hbm, near_hbm_out, sums_hbm,
    out_ref, chosen_ref, near_ref, emb, sent, col, parts, shares, ours, cand, least, share_ref,
    in_sem, zs, ps, os, bs, cs, ks, major_r, minor_r, sib_r, sum_sem,
):
    x, y, c, z = place()
    nz = lax.axis_size("dev")
    position = lax.axis_index("group") * nz + z
    rows = emb.shape[0] * 16
    slab = 4 * nz
    half = emb.shape[2] // 2
    cut = 3 * half // 4
    at_z, at_xy = z * 2 + c, x * NY + y
    major, minor = (y, x), (x, y)

    load = pltpu.make_async_copy(emb_hbm, emb, in_sem.at[0])
    load_chosen = pltpu.make_async_copy(chosen_hbm, chosen_ref, in_sem.at[1])
    load_near = pltpu.make_async_copy(near_hbm, near_ref, in_sem.at[2])
    load_chosen.start()
    load.start()
    load_near.start()

    column = [((z + dz) % nz, (c + dc) % 2) for dz, dc in far_first((nz, 2))]
    plane = [((x + dx) % NX, (y + dy) % NY) for dx, dy in PLANE]
    barrier = pltpu.get_barrier_semaphore()
    for tz, tc in column:
        pl.semaphore_signal(barrier, inc=1, device_id=device(x, y, tc, tz), device_id_type=MESH)
    for tx, ty in plane:
        pl.semaphore_signal(barrier, inc=1, device_id=device(tx, ty, c, z), device_id_type=MESH)

    least[...] = jnp.full(least.shape, jnp.inf, jnp.float32)
    load_chosen.wait()
    picks = find_picks(chosen_ref[...], position, rows)
    load.wait()
    found = picked_rows(picks, emb)
    for h in range(2):
        wide = found[:, half * h : half * (h + 1)]
        tail = jnp.concatenate([wide[4 * i : 4 * i + 4, cut:] for i in range(3)], axis=1)
        sent[h] = jnp.concatenate([wide[:, :cut], tail], axis=0).astype(jnp.bfloat16)
    col[at_z] = sent[c]
    pl.semaphore_wait(barrier, len(column) + len(plane))

    def remote(src, dst, ssem, rsem, target):
        return pltpu.make_async_remote_copy(
            src_ref=src, dst_ref=dst, send_sem=ssem, recv_sem=rsem,
            device_id=target, device_id_type=MESH)

    def drain(ref, sems):
        return remote(ref, ref, sems.at[0], sems.at[1], device(x, y, 1 - c, z))

    for tz, tc in column:
        remote(sent.at[tc], col.at[at_z], zs.at[0], zs.at[1], device(x, y, tc, tz)).start()
    slots = drain(col.at[pl.ds(0, len(column))], zs)

    for j in range(rows // 128):
        part = emb[8 * j : 8 * (j + 1)].reshape(128, -1).astype(jnp.float32)
        part = part * part
        part = sum(part[:, 128 * i : 128 * (i + 1)] for i in range(part.shape[1] // 128))
        out_ref[:, 128 * j : 128 * (j + 1)] = jnp.sum(part.T, axis=0, keepdims=True)

    main, tails = slot_sources(chosen_ref, x, y, z, rows, nz)
    slots.wait_recv()

    gathered = col[...].reshape(-1, cut)
    left = jnp.dot(main, gathered, preferred_element_type=jnp.float32)
    stacked = jnp.concatenate([gathered[:, 128 * i : 128 * (i + 1)] for i in range(3)], axis=0)
    right = jnp.dot(
        jnp.concatenate(tails, axis=1), stacked, preferred_element_type=jnp.float32
    )
    dense = jnp.concatenate([left, right], axis=1)
    for t in range(NX * NY):
        rows8 = dense[8 * t : 8 * t + 8]
        both = jnp.concatenate([rows8[:, : half // 2], rows8[:, half // 2 :]], axis=0)
        parts[t] = both.astype(jnp.bfloat16)
    shares[at_xy] = parts[at_xy]

    for tx, ty in plane:
        t = tx * NY + ty
        remote(parts.at[t], shares.at[at_xy], ps.at[0], ps.at[1], device(tx, ty, c, z)).start()
    part = drain(shares.at[pl.ds(0, len(plane))], ps)
    part.wait_recv()
    ours[z] = jnp.sum(shares[...].astype(jnp.float32), axis=0).astype(jnp.bfloat16)

    for k in (4, 3, 5, 2, 6, 1, 7):
        remote(ours.at[z], ours.at[z], os.at[0], os.at[1], device(x, y, c, (z + k) % nz)).start()
    along = drain(ours.at[pl.ds(0, nz - 1)], os)
    along.wait_recv()
    for p in range(2):
        rows8 = [ours[p * (nz // 2) + t].astype(jnp.float32) for t in range(nz // 2)]
        packed = [jnp.concatenate([r[:8], r[8:]], axis=1) for r in rows8]
        start = pl.multiple_of(minor[p] * slab, 16)
        cand[p, c, major[p], pl.ds(start, slab), :] = jnp.concatenate(packed, axis=0).astype(
            jnp.bfloat16
        )

    def slab_at(p, a, b, core, piece=None):
        start, size = (b * slab, slab) if piece is None else (b * slab + 16 * piece, 16)
        return cand.at[p, core, a, pl.ds(pl.multiple_of(start, 16), size), :]

    def spot(p, a, b):
        return (b, a) if p == 0 else (a, b)

    def copy(p, a, b, core, ssem, rsem, target, piece=None):
        ref = slab_at(p, a, b, core, piece)
        return remote(ref, ref, ssem, rsem, target)

    def major_copy(p, k, h):
        a, b = major[p], minor[p]
        tx, ty = spot(p, (a + k) % 4, b)
        return copy(p, a, b, c, bs.at[p], major_r.at[p, a, h], device(tx, ty, c, z), h)

    def minor_copy(p, a, k, h=None):
        b = minor[p]
        tx, ty = spot(p, major[p], (b + k) % 4)
        return copy(p, a, b, c, cs.at[p], minor_r.at[p, a], device(tx, ty, c, z), h)

    def core_copy(p, a):
        ref = cand.at[p, c, a]
        return remote(ref, ref, ks.at[p], sib_r.at[p, a], device(x, y, 1 - c, z))

    def major_arrival(p, a, h):
        return copy(p, a, minor[p], c, bs.at[p], major_r.at[p, a, h], device(x, y, 1 - c, z), h)

    def minor_arrivals(p, a):
        ref = cand.at[p, c, a, pl.ds(0, 3 * slab)]
        return remote(ref, ref, cs.at[p], minor_r.at[p, a], device(x, y, 1 - c, z))

    def core_arrival(p, a):
        ref = cand.at[p, 1 - c, a]
        return remote(ref, ref, ks.at[p], sib_r.at[p, a], device(x, y, 1 - c, z))

    for h in range(2):
        for k in (2, 1, 3):
            for p in range(2):
                major_copy(p, k, h).start()
    for p in range(2):
        for k in (2, 1, 3):
            minor_copy(p, major[p], k).start()
    for k, h in ((1, 0), (3, 0), (1, 1), (3, 1), (2, 0), (2, 1)):
        for p in range(2):
            a = (major[p] + k) % 4
            major_arrival(p, a, h).wait_recv()
            for j in (2, 1, 3):
                minor_copy(p, a, j, h).start()

    def pass_on(p, k):
        a = (major[p] + k) % 4
        minor_arrivals(p, a).wait_recv()
        core_copy(p, a).start()

    def absorb(k):
        at = [(major[p] + k) % 4 for p in range(2)]
        for p in range(2):
            core_arrival(p, at[p]).wait_recv()
        blocks = [jnp.concatenate([cand[p, h, at[p]] for p in range(2)], axis=0) for h in range(2)]
        wide = [block.astype(jnp.float32) for block in blocks]
        norm = jnp.sum(wide[0] * wide[0] + wide[1] * wide[1], axis=1, keepdims=True) * 0.25
        for j in range(rows // TILE):
            lanes = slice(TILE * j, TILE * (j + 1))
            mine = emb[TILE // 16 * j : TILE // 16 * (j + 1)].reshape(TILE, -1)
            product = sum(
                lax.dot_general(
                    blocks[h], mine[:, half * h : half * (h + 1)], NT,
                    preferred_element_type=jnp.float32)
                for h in range(2)
            )
            reach = jnp.min((product + norm).reshape(2, -1, 8, TILE), axis=1)
            least[:, :, lanes] = jnp.minimum(least[:, :, lanes], reach)

    def pass_both(k):
        for p in range(2):
            pass_on(p, k)

    pass_both(0)
    pass_both(1)
    absorb(0)
    pass_both(3)
    absorb(1)
    pass_both(2)
    absorb(3)
    absorb(2)
    load_near.wait()

    norms = out_ref[...]
    near = near_ref[...]
    sums = []
    for p in range(2):
        reach = jnp.min(least[p], axis=0, keepdims=True)
        near = jnp.minimum(near, jnp.maximum(norms + reach, 0.0))
        sums.append(jnp.sum(near, axis=1, keepdims=True))
    lane = lax.broadcasted_iota(jnp.int32, (1, 128), 1)
    share = jnp.where(lane == 0, sums[0], jnp.where(lane == 1, sums[1], 0.0))

    share_ref[...] = share
    mine_at = sums_hbm.at[pl.ds(position, 1)]
    keep = pltpu.make_async_copy(share_ref, mine_at, in_sem.at[1])
    everyone = far_first((NX, NY, nz, 2))
    xs, ys = [(x + i) % NX for i in range(NX)], [(y + i) % NY for i in range(NY)]
    zs_, cores = [(z + i) % nz for i in range(nz)], [c, 1 - c]
    for dx, dy, dz, dc in everyone:
        target = device(xs[dx], ys[dy], cores[dc], zs_[dz])
        remote(share_ref, mine_at, sum_sem.at[0], sum_sem.at[1], target).start()
    keep.start()
    out_ref[...] = near
    store = pltpu.make_async_copy(out_ref, near_hbm_out, in_sem.at[0])
    store.start()

    slots.wait_send()
    part.wait_send()
    along.wait_send()
    for p in range(2):
        three = cand.at[p, c, pl.ds(0, 3)]
        first = cand.at[p, c, 0, pl.ds(0, 3 * slab)]
        remote(first, first, bs.at[p], major_r.at[p, 0, 0], device(x, y, 1 - c, z)).wait_send()
        remote(three, three, cs.at[p], minor_r.at[p, 0], device(x, y, 1 - c, z)).wait_send()
        four = cand.at[p, c]
        remote(four, four, ks.at[p], sib_r.at[p, 0], device(x, y, 1 - c, z)).wait_send()
    others = sums_hbm.at[pl.ds(0, len(everyone))]
    both = remote(others, others, sum_sem.at[0], sum_sem.at[1], device(x, y, 1 - c, z))
    keep.wait()
    store.wait()
    both.wait_send()
    both.wait_recv()


def finish(near_in, sums_in, near_out, cost_out, near_ref, sums_ref, sem, *, total_rows):
    near_load = pltpu.make_async_copy(near_in, near_ref, sem.at[0])
    sums_load = pltpu.make_async_copy(sums_in, sums_ref, sem.at[1])
    near_store = pltpu.make_async_copy(near_ref, near_out, sem.at[2])
    sums_load.start()
    near_load.start()
    near_load.wait()
    near_store.start()
    sums_load.wait()
    total = jnp.sum(sums_ref[...], axis=0, keepdims=True) / total_rows
    cost_out[0] = total[0, 0]
    cost_out[1] = total[0, 1]
    near_store.wait()


def local(embeddings, nearest, chosen):
    rows, width = embeddings.shape
    nz = lax.axis_size("dev")
    total_rows = rows * nz * lax.axis_size("group")
    dma = pltpu.SemaphoreType.DMA

    near, sums = pl.pallas_call(
        kernel,
        out_shape=(
            jax.ShapeDtypeStruct((1, rows), jnp.float32),
            jax.ShapeDtypeStruct((total_rows // rows, 128), jnp.float32),
        ),
        in_specs=[
            pl.BlockSpec(memory_space=pl.ANY),
            pl.BlockSpec(memory_space=pl.ANY),
            pl.BlockSpec(memory_space=pl.ANY),
        ],
        out_specs=(
            pl.BlockSpec(memory_space=pl.ANY),
            pl.BlockSpec(memory_space=pl.ANY),
        ),
        scratch_shapes=[
            pltpu.VMEM((1, rows), jnp.float32),
            pltpu.VMEM(chosen.shape, jnp.int32),
            pltpu.VMEM((1, rows), jnp.float32),
            pltpu.VMEM((rows // 16, 16, width), jnp.bfloat16),
            pltpu.VMEM((2, 16, 3 * width // 8), jnp.bfloat16),
            pltpu.VMEM((2 * nz, 16, 3 * width // 8), jnp.bfloat16),
            pltpu.VMEM((NX * NY, 16, width // 4), jnp.bfloat16),
            pltpu.VMEM((NX * NY, 16, width // 4), jnp.bfloat16),
            pltpu.VMEM((nz, 16, width // 4), jnp.bfloat16),
            pltpu.VMEM((2, 2, 4, 16 * nz, width // 2), jnp.bfloat16),
            pltpu.VMEM((2, 8, rows), jnp.float32),
            pltpu.VMEM((1, 128), jnp.float32),
            dma((3,)),
            dma((2,)),
            dma((2,)),
            dma((2,)),
            dma((2,)),
            dma((2,)),
            dma((2,)),
            dma((2, 4, 2)),
            dma((2, 4)),
            dma((2, 4)),
            dma((2,)),
        ],
        compiler_params=pltpu.CompilerParams(
            collective_id=0, has_side_effects=True, vmem_limit_bytes=60 * 2**20
        ),
        cost_estimate=pl.CostEstimate(
            flops=4 * rows * width * chosen.shape[1], bytes_accessed=rows * width * 2, transcendentals=0
        ),
    )(chosen, nearest.reshape(1, rows), embeddings.reshape(rows // 16, 16, width))
    near, cost = pl.pallas_call(
        functools.partial(finish, total_rows=total_rows),
        out_shape=(
            jax.ShapeDtypeStruct((1, rows), jnp.float32),
            jax.ShapeDtypeStruct((2,), jnp.float32),
        ),
        in_specs=[
            pl.BlockSpec(memory_space=pl.ANY),
            pl.BlockSpec(memory_space=pl.ANY),
        ],
        out_specs=(
            pl.BlockSpec(memory_space=pl.ANY),
            pl.BlockSpec(memory_space=pltpu.SMEM),
        ),
        scratch_shapes=[
            pltpu.VMEM((1, rows), jnp.float32),
            pltpu.VMEM((total_rows // rows, 128), jnp.float32),
            dma((3,)),
        ],
        compiler_params=pltpu.CompilerParams(vmem_limit_bytes=60 * 2**20),
    )(near, sums)
    return near.reshape(rows), cost


def solution(mesh):
    return jax.shard_map(
        local,
        mesh=mesh,
        in_specs=(P(("group", "dev"), None), P(("group", "dev")), P()),
        out_specs=(P(("group", "dev")), P()),
        check_vma=False,
    )
```
